128 devices in a mesh: ctx: 32 (over x, z, core), head: 4 (over y).
Axes of the slice: x: 4, y: 4, z: 4, core: 2. Of those that a mesh axis runs over, the one named last changes fastest.
Arguments:
- queries: bfloat16 [16384, 2560], P(('ctx', 'head')), may hold values from -6 to 6
- key_rows: bfloat16 [16384, 2560], P(('ctx', 'head')), may hold values from -6 to 6
- value_rows: bfloat16 [16384, 2560], P(('ctx', 'head')), may hold values from -6 to 6
- forward_out: bfloat16 [16384, 2560], P(('ctx', 'head')), may hold values from -6 to 6
- out_grad: bfloat16 [16384, 2560], P(('ctx', 'head')), may hold values from -96 to 96
- log_norm: float32 [16384, 20], P(('ctx', 'head')), may hold values from -1 to 12
- block_order: int32 [128], replicated, may hold values from 0 to 127, as said below
- pattern: int32 [128, 36], replicated, may hold values from -1 to 127, as said below
Outputs:
- query_grad: bfloat16 [16384, 2560], P(('ctx', 'head'))
- key_grad: bfloat16 [16384, 2560], P(('ctx', 'head'))
- value_grad: bfloat16 [16384, 2560], P(('ctx', 'head'))
The draws below stay inside these ranges and needn't reach their ends.
Inputs may be any that keep to these rules, and one draw needn't show every extreme that they name: `block_order`: A permutation of the block numbers. `pattern`: row g names each key block at most once, -1 marks an unused entry, and g itself is always named. Among the blocks stored on any one index of ctx, the query blocks stored on another index name at most one block, and when one of those query blocks names it, all of them do; the query blocks of every index name one block stored on the next index of ctx (cyclically).
All inputs are finite; a program needn't handle non-finite values.
Results may differ from the reference program's by a relative error of at most 0.0062.
Values may be sent and summed in bfloat16 or wider, within the bound.
A program may use at most 192 MiB of HBM per device.

```python
import jax
import jax.numpy as jnp
from jax import lax

HEADS = 20
HD = 128
BLK = 128
D = 2560
TOKENS = 16384
BLOCKS = 128
QB_DEV = 4
NNZ = 36
N_CTX = 32


def shared_layout(key):
    order = jax.random.permutation(jax.random.fold_in(key, 101), BLOCKS).astype(jnp.int32)
    level = jax.random.randint(jax.random.fold_in(key, 102), (N_CTX, 1), 1, 5)
    coin = jax.random.randint(jax.random.fold_in(key, 103), (N_CTX, N_CTX), 0, 4)
    peers = jnp.arange(N_CTX, dtype=jnp.int32)
    numbers = jnp.arange(QB_DEV, dtype=jnp.int32)
    following = (peers[:, None] + 1) % N_CTX == peers[None, :]
    needed = ((coin < level) | following) & (peers[:, None] != peers[None, :])
    pick = jax.random.randint(jax.random.fold_in(key, 104), (N_CTX, N_CTX), 0, QB_DEV)
    local = jax.random.randint(jax.random.fold_in(key, 106), (N_CTX, QB_DEV, QB_DEV), 0, 2) == 1
    local = local | (numbers[:, None] == numbers[None, :])[None, :, :]
    local_slot = jnp.where(local, peers[:, None, None] * QB_DEV + numbers[None, None, :], -1)
    remote_ok = jnp.broadcast_to(needed[:, None, :], (N_CTX, QB_DEV, N_CTX))
    remote_slot = jnp.where(remote_ok, peers[None, None, :] * QB_DEV + pick[:, None, :], -1)
    slots = jnp.concatenate([local_slot, remote_slot], axis=-1).reshape(BLOCKS, NNZ)
    globals_listed = jnp.where(slots >= 0, order[jnp.maximum(slots, 0)], -1)
    table = jnp.zeros((BLOCKS, NNZ), jnp.int32).at[order].set(globals_listed)
    row_keys = jax.random.split(jax.random.fold_in(key, 107), BLOCKS)
    table = jax.vmap(lambda row_key, row: jax.random.permutation(row_key, row))(row_keys, table)
    return (order, table.astype(jnp.int32))


def draw_block_order(key, part):
    order, table = shared_layout(key)
    return order


def draw_pattern(key, part):
    order, table = shared_layout(key)
    return table


def draw_log_norm(key, part):
    order, table = shared_layout(key)
    key = jax.random.fold_in(key, 7)
    listed = jnp.sum((table >= 0).astype(jnp.int32), axis=-1)
    per_slot = listed[order]
    inner = jnp.arange(TOKENS, dtype=jnp.int32) % BLK
    count = (jnp.repeat(per_slot, BLK) - 1) * BLK + inner + 1
    base = jnp.log(count.astype(jnp.float32)) + 0.5
    return base[:, None] + jax.random.uniform(key, (TOKENS, HEADS), jnp.float32, -0.75, 0.75)


def block_scale(stream_key, dims, shards, least, high):
    gain = 1.0
    for dim, blocks in shards:
        steps = jax.random.uniform(jax.random.fold_in(jax.random.fold_in(stream_key, 6), dim), (blocks,), jnp.float32, least / len(shards), high / len(shards))
        gain = gain * jnp.repeat(jnp.exp(steps), dims[dim] // blocks).reshape((-1,) + (1,) * (len(dims) - 1 - dim))
    return gain


def noise(own_key, shape, spread, bound, cuts=(), kind=jnp.bfloat16):
    level = block_scale(own_key, shape, cuts, -0.22, 0.18) if cuts else 1.0
    array = jax.random.normal(own_key, shape, jnp.float32) * spread * level
    return jnp.minimum(jnp.maximum(array, -bound), bound).astype(kind)


def setup_inputs(seed: int = 0) -> dict:
    keys = jax.random.split(jax.random.key(seed), 9)
    queries = noise(keys[0], (TOKENS, D), 1.0, 6.0, ((0, 128),))
    key_rows = noise(keys[1], (TOKENS, D), 1.0, 6.0, ((0, 128),))
    value_rows = noise(keys[2], (TOKENS, D), 1.0, 6.0, ((0, 128),))
    forward_out = noise(keys[3], (TOKENS, D), 1.0, 6.0, ((0, 128),))
    out_grad = noise(keys[4], (TOKENS, D), 16.0, 96.0, ((0, 128),))
    log_norm = draw_log_norm(jax.random.fold_in(keys[8], 71), 0)
    block_order = draw_block_order(jax.random.fold_in(keys[8], 71), 0)
    pattern = draw_pattern(jax.random.fold_in(keys[8], 71), 0)
    return {"queries": queries, "key_rows": key_rows, "value_rows": value_rows, "forward_out": forward_out, "out_grad": out_grad, "log_norm": log_norm, "block_order": block_order, "pattern": pattern}


def adjacency(block_order, pattern):
    blocks = block_order.shape[0]
    numbers = jnp.arange(blocks, dtype=jnp.int32)
    slot_of = jnp.zeros((blocks,), jnp.int32).at[block_order.astype(jnp.int32)].set(numbers)
    listed = pattern[block_order.astype(jnp.int32)]
    key_slot = jnp.where(listed >= 0, slot_of[jnp.maximum(listed, 0).astype(jnp.int32)], -1)
    return jnp.any(key_slot[:, :, None] == numbers[None, None, :], axis=1)


def reference(queries, key_rows, value_rows, forward_out, out_grad, log_norm, block_order, pattern):
    width = HEADS * HD
    rows_mine = QB_DEV * BLK
    scale = HD ** -0.5
    adjacent = adjacency(block_order, pattern).reshape(N_CTX, QB_DEV, N_CTX, QB_DEV)
    numbers = jnp.arange(QB_DEV, dtype=jnp.int32)
    peers = jnp.arange(N_CTX, dtype=jnp.int32)
    offdiag = (peers[:, None] != peers[None, :])[:, :, None]
    pick_all = jnp.sum(jnp.where(jnp.any(adjacent, axis=1) & offdiag, numbers[None, None, :], 0), axis=-1).astype(jnp.int32)
    rowdot = jnp.sum((out_grad.astype(jnp.float32) * forward_out.astype(jnp.float32)).reshape(TOKENS, HEADS, HD), axis=-1)
    query4 = queries.reshape(N_CTX, rows_mine, HEADS, HD)
    grad4 = out_grad.reshape(N_CTX, rows_mine, HEADS, HD)
    key_blocks = key_rows.reshape(N_CTX, QB_DEV, BLK, HEADS, HD)
    value_blocks = value_rows.reshape(N_CTX, QB_DEV, BLK, HEADS, HD)
    norm3 = log_norm.reshape(N_CTX, rows_mine, HEADS)
    dot3 = rowdot.reshape(N_CTX, rows_mine, HEADS)
    position = jnp.arange(rows_mine, dtype=jnp.int32)
    same_block = (position[:, None] // BLK) == (position[None, :] // BLK)
    causal = jnp.logical_or(jnp.logical_not(same_block), position[:, None] >= position[None, :])

    def per_device(carry, index):
        acc_k, acc_v = carry
        pick = pick_all[index]
        mine = adjacent[index]
        own = mine[:, index, :]
        local_mask = jnp.repeat(jnp.repeat(own, BLK, axis=0), BLK, axis=1) & causal
        chosen = numbers[None, :] == pick[:, None]
        remote = jnp.any(mine & chosen[None, :, :], axis=-1) & (peers != index)[None, :]
        remote_mask = jnp.repeat(jnp.repeat(remote, BLK, axis=0), BLK, axis=1)
        mask = jnp.concatenate([local_mask, remote_mask], axis=1)
        keys_far = key_blocks[peers, pick].reshape(N_CTX * BLK, HEADS, HD)
        values_far = value_blocks[peers, pick].reshape(N_CTX * BLK, HEADS, HD)
        pool_k = jnp.concatenate([key_blocks[index].reshape(rows_mine, HEADS, HD), keys_far], axis=0)
        pool_v = jnp.concatenate([value_blocks[index].reshape(rows_mine, HEADS, HD), values_far], axis=0)
        query_c = query4[index]
        grad_c = grad4[index]
        norm_c = norm3[index]
        dot_c = dot3[index]

        def one_head(head):
            query_h = query_c[:, head]
            grad_h = grad_c[:, head]
            key_h = pool_k[:, head]
            value_h = pool_v[:, head]
            score = jnp.dot(query_h, key_h.T, preferred_element_type=jnp.float32) * scale
            prob = jnp.where(mask, jnp.exp(score - norm_c[:, head][:, None]), 0.0)
            dprob = jnp.dot(grad_h, value_h.T, preferred_element_type=jnp.float32)
            dscore = (prob * (dprob - dot_c[:, head][:, None])).astype(jnp.bfloat16)
            probs = prob.astype(jnp.bfloat16)
            return (jnp.dot(dscore, key_h, preferred_element_type=jnp.float32) * scale,
                    jnp.dot(dscore.T, query_h, preferred_element_type=jnp.float32) * scale,
                    jnp.dot(probs.T, grad_h, preferred_element_type=jnp.float32))

        dq_h, dk_h, dv_h = lax.map(one_head, jnp.arange(HEADS, dtype=jnp.int32))
        dq = jnp.transpose(dq_h, (1, 0, 2)).reshape(rows_mine, width)
        dk = jnp.transpose(dk_h, (1, 0, 2)).reshape(rows_mine + N_CTX * BLK, width)
        dv = jnp.transpose(dv_h, (1, 0, 2)).reshape(rows_mine + N_CTX * BLK, width)
        far_k = lax.optimization_barrier(dk[rows_mine:].reshape(N_CTX, BLK, width).astype(jnp.bfloat16))
        far_v = lax.optimization_barrier(dv[rows_mine:].reshape(N_CTX, BLK, width).astype(jnp.bfloat16))
        slots = (peers * QB_DEV + pick).astype(jnp.int32)
        acc_k = acc_k.at[slots].add(far_k.astype(jnp.float32))
        acc_v = acc_v.at[slots].add(far_v.astype(jnp.float32))
        return (acc_k, acc_v), (dq, dk[:rows_mine], dv[:rows_mine])

    start = (jnp.zeros((BLOCKS, BLK, width), jnp.float32), jnp.zeros((BLOCKS, BLK, width), jnp.float32))
    (acc_k, acc_v), (dq, dk_local, dv_local) = lax.scan(per_device, start, jnp.arange(N_CTX, dtype=jnp.int32))
    query_grad = dq.reshape(TOKENS, width).astype(jnp.bfloat16)
    key_grad = (dk_local.reshape(TOKENS, width) + acc_k.reshape(TOKENS, width)).astype(jnp.bfloat16)
    value_grad = (dv_local.reshape(TOKENS, width) + acc_v.reshape(TOKENS, width)).astype(jnp.bfloat16)
    return (query_grad, key_grad, value_grad)
```

```python
import functools

import jax
import jax.numpy as jnp
from jax import lax
from jax.experimental import pallas as pl
from jax.experimental.pallas import tpu as pltpu
from jax.sharding import PartitionSpec as P

MESH = pl.DeviceIdType.MESH
HBM = pl.ANY
VMEM = pltpu.VMEM
BF = jnp.bfloat16
F32 = jnp.float32
BLK = 128
HEADS = 20
LOG2E = 1.4426950408889634
SCALE = 128 ** -0.5
FAR = 1e30
GROUP = 4 * BLK


def coords():
    c = lax.axis_index("ctx")
    return c // 8, (c // 2) % 4, c % 2, lax.axis_index("head")


def dev(x, z, k, y):
    return (x * 8 + z * 2 + k, y)


def rows(start, size):
    return pl.ds(pl.multiple_of(start, BLK), size)


def cols(head):
    return pl.ds(pl.multiple_of(head * BLK, BLK), BLK)


def q_pair(z):
    return z + 1 - 2 * (z % 2)


def k_pair(z):
    return (z + 3 + 2 * (z % 2)) % 4


def send(src, dst, ss, rs, to):
    pltpu.make_async_remote_copy(
        src_ref=src, dst_ref=dst, send_sem=ss, recv_sem=rs, device_id=to, device_id_type=MESH
    ).start()


def wait(ref, sem):
    pltpu.make_async_copy(ref, ref, sem).wait()


def greet():
    x, z, k, y = coords()
    barrier = pltpu.get_barrier_semaphore()
    peers = [dev((x + dx) % 4, z, k, (y + dy) % 4) for dx in range(4) for dy in range(4) if dx or dy]
    peers += [dev(x, (z + dz) % 4, k, y) for dz in range(1, 4)]
    peers.append(dev(x, z, 1 - k, y))
    for peer in peers:
        pl.semaphore_signal(barrier, inc=1, device_id=peer, device_id_type=MESH)
    pl.semaphore_wait(barrier, len(peers))


DX = (0, 1, 3, 2)


def gather_kernel(
    q_in, k_in, v_in, g_in, o_in, norm_in, pat_in, order_in,
    qa, ga, xa, ka, va, qb, gb, xb, kb, vb, table,
    g_v, o_v, aux, square, pat_v,
    load_sem, sa1, ra1, sb1, rb1, s_zq, r_zq, s_c, r_c, s_c2, r_c2, s_zk, r_zk,
    s_bz, r_bz, s_bc, r_bc, s_bx, r_bx,
):
    x, z, k, y = coords()
    load_g = pltpu.make_async_copy(g_in, g_v, load_sem.at[0])
    load_o = pltpu.make_async_copy(o_in, o_v, load_sem.at[1])
    load_g.start()
    load_o.start()
    greet()
    mine = (x * 4 + y) * BLK

    wide = ((0, q_in, qa, qb), (1, g_in, ga, gb), (2, k_in, ka, kb), (3, v_in, va, vb))

    def scatter_a(a, src_of, dst, n):
        for dx in DX:
            for dy in range(4):
                tx, ty = (x + dx) % 4, (y + dy) % 4
                src = src_of(ty * 4 + tx)
                if dx or dy:
                    send(src, dst, sa1.at[a], ra1.at[a, dx], dev(tx, z, k, ty))
                else:
                    pltpu.make_async_copy(src, dst, ra1.at[a, 0]).start()

    def scatter_b(a, src_of, dst_of):
        for dy in range(4):
            ty = (y + dy) % 4
            src = src_of(16 + ty)
            if dy:
                send(src, dst_of, sb1.at[a], rb1.at[a], dev(x, z, k, ty))
            else:
                pltpu.make_async_copy(src, dst_of, rb1.at[a]).start()

    slot = k * 4 + z
    for a, src, da, db in wide:
        scatter_a(a, lambda h, src=src: src.at[:, cols(h)], da.at[rows(mine, BLK), :], BLK)
        base = (slot if a < 2 else x) * GROUP + y * BLK
        scatter_b(a, lambda h, src=src: src.at[:, cols(h)], db.at[rows(base, BLK), :])

    square[...] = jnp.zeros((BLK, BLK), F32)
    square[:, 0:HEADS] = norm_in[...] * LOG2E
    norm_t = square[...].T
    load_g.wait()
    load_o.wait()
    for h in range(HEADS):
        prod = g_v[:, h * BLK:(h + 1) * BLK].astype(F32) * o_v[:, h * BLK:(h + 1) * BLK].astype(F32)
        dot = jnp.sum(prod.T, axis=0, keepdims=True)
        aux[h] = jnp.concatenate([norm_t[h:h + 1], dot, jnp.zeros((6, BLK), F32)], axis=0)
    scatter_a(4, lambda h: aux.at[h], xa.at[x * 4 + y], 1)
    scatter_b(4, lambda h: aux.at[h], xb.at[slot * 4 + y])

    def part(a, ref, quad, dx, count=4):
        xs = (x + 4 - dx) % 4
        if a == 4:
            return ref.at[pl.ds((quad * 4 + xs) * 4, 4)]
        return ref.at[rows((quad * 4 + xs) * GROUP, GROUP), :]

    buf_a = {0: qa, 1: ga, 2: ka, 3: va, 4: xa}
    buf_b = {0: qb, 1: gb, 2: kb, 3: vb, 4: xb}
    to_q = dev(x, q_pair(z), k, y)
    to_k = dev(x, k_pair(z), k, y)
    to_c = dev(x, z, 1 - k, y)

    def forward_a(dx):
        for a in (0, 1, 4):
            ref = buf_a[a]
            wait(part(a, ref, 0, dx), ra1.at[a, dx])
            send(part(a, ref, 0, dx), part(a, ref, 1, dx), s_zq.at[a], r_zq.at[a, dx], to_q)
            send(part(a, ref, 0, dx), part(a, ref, 2, dx), s_c.at[a], r_c.at[a], to_c)
        for a in (2, 3):
            ref = buf_a[a]
            wait(part(a, ref, 0, dx), ra1.at[a, dx])
            send(part(a, ref, 0, dx), part(a, ref, 1, dx), s_zk.at[a - 2], r_zk.at[a - 2], to_k)

    def slab(a, ref, index, count=1):
        if a == 4:
            return ref.at[pl.ds(index * 4, 4 * count)]
        return ref.at[rows(index * GROUP, GROUP * count), :]

    def forward_b():
        for a in (0, 1, 4):
            ref = buf_b[a]
            own = slab(a, ref, slot)
            wait(own, rb1.at[a])
            for dz in (1, 3, 2):
                send(own, own, s_bz.at[a], r_bz.at[a, dz], dev(x, (z + dz) % 4, k, y))
            send(own, own, s_bc.at[a], r_bc.at[a], to_c)
        for a in (2, 3):
            ref = buf_b[a]
            own = slab(a, ref, x)
            wait(own, rb1.at[a])
            for dx in (1, 3, 2):
                send(own, own, s_bx.at[a - 2], r_bx.at[a - 2], dev((x + dx) % 4, z, k, y))

    forward_a(0)
    forward_b()
    for dx in DX[1:]:
        forward_a(dx)

    pat_v[...] = jnp.full((BLK, BLK), -1.0, F32)
    pat_v[:, 0:36] = pat_in[...].astype(F32)
    order = order_in[...].astype(F32)
    i0 = lax.broadcasted_iota(jnp.int32, (BLK, BLK), 0)
    i1 = lax.broadcasted_iota(jnp.int32, (BLK, BLK), 1)
    hot = jnp.where(i0.astype(F32) == order, 1.0, 0.0).T
    listed = jnp.dot(hot.astype(BF), pat_v[...].astype(BF), preferred_element_type=F32)
    adj = jnp.zeros((BLK, BLK), F32)
    for e in range(36):
        adj = jnp.maximum(adj, jnp.where(listed[:, e:e + 1] == order, 1.0, 0.0))
    local = (i0 // 4) == (i1 // 4)
    pick = jnp.where((i0 // 4) == i1, (i0 % 4 + 1).astype(F32), 0.0)
    own_cols = jnp.where(i1 == 32 + i0 % 4, 1.0, 0.0)
    table[...] = (
        jnp.dot(jnp.where(local, 0.0, adj).astype(BF), pick.astype(BF), preferred_element_type=F32)
        + jnp.dot(jnp.where(local, adj, 0.0).astype(BF), own_cols.astype(BF), preferred_element_type=F32)
    ).astype(jnp.int32)

    for dz in (1, 3, 2):
        for a in (0, 1, 4):
            ref = buf_b[a]
            got = slab(a, ref, k * 4 + (z + 4 - dz) % 4)
            wait(got, r_bz.at[a, dz])
            send(got, got, s_bc.at[a], r_bc.at[a], to_c)
    for dx in DX:
        for a in (0, 1, 4):
            ref = buf_a[a]
            wait(part(a, ref, 1, dx), r_zq.at[a, dx])
            send(part(a, ref, 1, dx), part(a, ref, 3, dx), s_c2.at[a], r_c2.at[a], to_c)

    def quad(a, ref, index):
        if a == 4:
            return ref.at[pl.ds(index * 16, 16)]
        return ref.at[pl.ds(index * 4 * GROUP, 4 * GROUP), :]

    for a in (2, 3):
        wait(quad(a, buf_a[a], 1), r_zk.at[a - 2])
        wait(quad(a, buf_a[a], 0), s_zk.at[a - 2])
        wait(slab(a, buf_b[a], 0, 3), r_bx.at[a - 2])
        wait(slab(a, buf_b[a], 0, 3), s_bx.at[a - 2])
    for a in (0, 1, 4):
        wait(quad(a, buf_a[a], 2), r_c.at[a])
        wait(quad(a, buf_a[a], 3), r_c2.at[a])
        wait(quad(a, buf_a[a], 0), s_zq.at[a])
        wait(quad(a, buf_a[a], 0), s_c.at[a])
        wait(quad(a, buf_a[a], 0), s_c2.at[a])
        wait(slab(a, buf_b[a], 0, 4), r_bc.at[a])
        wait(slab(a, buf_b[a], 0, 4), s_bc.at[a])
        wait(slab(a, buf_b[a], 0, 3), s_bz.at[a])
    for a in range(5):
        ref = buf_a[a]
        if a == 4:
            wait(ref.at[pl.ds(0, 15)], sa1.at[a])
            wait(ref.at[pl.ds(0, 3)], sb1.at[a])
        else:
            wait(ref.at[pl.ds(0, 15 * BLK), :], sa1.at[a])
            wait(ref.at[pl.ds(0, 3 * BLK), :], sb1.at[a])


def against_rows(left, right):
    return lax.dot_general(left, right, (((1,), (1,)), ((), ())), preferred_element_type=F32)


def against_cols(left, right):
    return lax.dot_general(left, right, (((0,), (0,)), ((), ())), preferred_element_type=F32)


def compute_kernel(
    table, qa, ga, xa, ka, va, qb, gb, xb, kb, vb,
    dqa, dka, dva, dqb, dkb, dvb,
    acc_k, acc_v, dq_acc,
):
    x, z, k, y = coords()
    base2 = SCALE * LOG2E

    def one_pass(query, grad, norm, dot, keys, values, biases, causal):
        score = against_rows(keys, query)
        dprob = against_rows(values, grad)
        probs, scores = [], []
        for i in range(4):
            cut = slice(i * BLK, (i + 1) * BLK)
            prob = jnp.exp2(score[cut] * base2 - (norm + biases[i]))
            if causal:
                key_at = lax.broadcasted_iota(jnp.int32, (BLK, GROUP), 0)
                query_at = lax.broadcasted_iota(jnp.int32, (BLK, GROUP), 1) - i * BLK
                hidden = (query_at >= 0) & (query_at < key_at)
                prob = jnp.where(hidden, 0.0, prob)
            probs.append(prob.astype(BF))
            scores.append((prob * (dprob[cut] - dot)).astype(BF))
        prob = jnp.concatenate(probs, axis=0)
        score = jnp.concatenate(scores, axis=0)
        return (
            against_cols(score, keys),
            jnp.dot(score, query, preferred_element_type=F32),
            jnp.dot(prob, grad, preferred_element_type=F32),
        )

    def run(q_ref, g_ref, x_ref, k_ref, v_ref, dq_ref, q, c, key_groups, diag):
        at = pl.ds(pl.multiple_of(q * GROUP, GROUP), GROUP)
        query, grad = q_ref[at, :], g_ref[at, :]
        norm = jnp.concatenate([x_ref[q * 4 + b, 0:1, :] for b in range(4)], axis=1)
        dot = jnp.concatenate([x_ref[q * 4 + b, 1:2, :] for b in range(4)], axis=1)
        total = None
        for first, key_index in key_groups:
            places, biases = [], []
            for i in range(4):
                code = table[4 * c, key_index(i)]
                places.append(pl.multiple_of((first + i) * GROUP + jnp.maximum(code - 1, 0) * BLK, BLK))
                biases.append(jnp.where(code > 0, 0.0, FAR))
            keys = jnp.concatenate([k_ref[pl.ds(p, BLK), :] for p in places], axis=0)
            values = jnp.concatenate([v_ref[pl.ds(p, BLK), :] for p in places], axis=0)
            dq, dk, dv = one_pass(query, grad, norm, dot, keys, values, biases, False)
            for i, p in enumerate(places):
                acc_k[pl.ds(p, BLK), :] += dk[i * BLK:(i + 1) * BLK]
                acc_v[pl.ds(p, BLK), :] += dv[i * BLK:(i + 1) * BLK]
            total = dq if total is None else total + dq
        dq_acc[...] = total
        pred, own = diag

        @pl.when(pred)
        def _():
            here = pl.ds(pl.multiple_of(own * GROUP, GROUP), GROUP)
            biases = [
                jnp.concatenate(
                    [
                        jnp.full((1, BLK), jnp.where(table[4 * c + b, 32 + i] > 0, 0.0, FAR), F32)
                        for b in range(4)
                    ],
                    axis=1,
                )
                for i in range(4)
            ]
            dq, dk, dv = one_pass(query, grad, norm, dot, k_ref[here, :], v_ref[here, :], biases, True)
            acc_k[here, :] += dk
            acc_v[here, :] += dv
            dq_acc[...] += dq

        dq_ref[at, :] = (dq_acc[...] * SCALE).astype(BF)

    def finish(dk_ref, dv_ref, n):
        def step(i, carry):
            at = pl.ds(pl.multiple_of(i * GROUP, GROUP), GROUP)
            dk_ref[at, :] = (acc_k[at, :] * SCALE).astype(BF)
            dv_ref[at, :] = acc_v[at, :].astype(BF)
            acc_k[at, :] = jnp.zeros((GROUP, BLK), F32)
            acc_v[at, :] = jnp.zeros((GROUP, BLK), F32)
            return carry

        lax.fori_loop(0, n, step, 0)

    acc_k[...] = jnp.zeros_like(acc_k)
    acc_v[...] = jnp.zeros_like(acc_v)
    zq, zk = q_pair(z), k_pair(z)

    def step_a(q, carry):
        quad, xq = q // 4, q % 4
        zc = jnp.where(quad % 2 == 0, z, zq)
        kc = jnp.where(quad < 2, k, 1 - k)
        c = xq * 8 + zc * 2 + kc
        groups = [
            (0, lambda i: i * 8 + z * 2 + k),
            (4, lambda i: i * 8 + zk * 2 + k),
        ]
        run(qa, ga, xa, ka, va, dqa, q, c, groups, (q < 4, q % 4))
        return carry

    lax.fori_loop(0, 16, step_a, 0)
    finish(dka, dva, 8)

    def step_b(q, carry):
        kc, zc = q // 4, q % 4
        c = x * 8 + zc * 2 + kc
        run(qb, gb, xb, kb, vb, dqb, q, c, [(0, lambda i: i * 8 + z * 2 + k)], (q == k * 4 + z, x))
        return carry

    lax.fori_loop(0, 8, step_b, 0)
    finish(dkb, dvb, 4)


def return_kernel(
    dqa, dka, dva, dqb, dkb, dvb,
    dq_out, dk_out, dv_out,
    got_zk, got_c, got_zq, put_zq, fin, bgot_c, bput_q, bgot_z, bgot_x, bfin,
    s_zk, r_zk, s_c, r_c, s_zq, r_zq, s_bc, r_bc, s_bz, r_bz, s_bx, r_bx, s_out, r_out,
):
    x, z, k, y = coords()
    outs = (dq_out, dk_out, dv_out)
    to_q = dev(x, q_pair(z), k, y)
    to_k = dev(x, k_pair(z), k, y)
    to_c = dev(x, z, 1 - k, y)
    greet()

    def chunk(ref, quad, dx):
        return ref.at[rows((quad * 4 + (x + dx) % 4) * GROUP, GROUP), :]

    def slab(ref, index):
        return ref.at[rows(index * GROUP, GROUP), :]

    for dx in DX:
        send(chunk(dqa, 3, dx), chunk(got_c, 1, dx), s_c, r_c.at[1, dx], to_c)
    send(dqb.at[rows((1 - k) * 4 * GROUP, 4 * GROUP), :], bgot_c, s_bc, r_bc, to_c)
    for dx in DX:
        for n, src in enumerate((dka, dva)):
            send(chunk(src, 1, dx), chunk(got_zk.at[n], 0, dx), s_zk, r_zk.at[n, dx], to_k)
    for dx in DX:
        send(chunk(dqa, 2, dx), chunk(got_c, 0, dx), s_c, r_c.at[0, dx], to_c)
    for dx in (1, 3, 2):
        for n, src in enumerate((dkb, dvb)):
            send(slab(src, (x + dx) % 4), slab(bgot_x.at[n], dx - 1), s_bx, r_bx.at[n, dx - 1], dev((x + dx) % 4, z, k, y))

    def add(*refs):
        total = refs[0][...].astype(F32)
        for ref in refs[1:]:
            total = total + ref[...].astype(F32)
        return total.astype(BF)

    for dx in DX:
        wait(chunk(got_c, 1, dx), r_c.at[1, dx])
        part = chunk(put_zq, 0, dx)
        part[...] = add(chunk(dqa, 1, dx), chunk(got_c, 1, dx))
        send(part, chunk(got_zq, 0, dx), s_zq, r_zq.at[dx], to_q)
    wait(bgot_c, r_bc)
    for dz in (1, 3, 2):
        zt = (z + dz) % 4
        part = slab(bput_q, zt)
        part[...] = add(slab(dqb, k * 4 + zt), slab(bgot_c, zt))
        send(part, slab(bgot_z, dz - 1), s_bz, r_bz.at[dz - 1], dev(x, zt, k, y))

    def give(n, src, base, tx, head_of, dx):
        for dy in range(4):
            ty = (y + dy) % 4
            block = src.at[rows(base + ty * BLK, BLK), :]
            dst = outs[n].at[:, cols(head_of)]
            if dx or dy:
                send(block, dst, s_out.at[n], r_out.at[n], dev(tx, z, k, ty))
            else:
                pltpu.make_async_copy(block, dst, r_out.at[n]).start()

    for dx in (1, 3, 2, 0):
        tx = (x + dx) % 4
        for n, own in ((1, dka), (2, dva)):
            wait(chunk(got_zk.at[n - 1], 0, dx), r_zk.at[n - 1, dx])
            out = chunk(fin.at[n], 0, dx)
            out[...] = add(chunk(own, 0, dx), chunk(got_zk.at[n - 1], 0, dx))
            give(n, fin.at[n], tx * GROUP, tx, y * 4 + x, dx)
    for dx in (1, 3, 2, 0):
        tx = (x + dx) % 4
        wait(chunk(got_c, 0, dx), r_c.at[0, dx])
        wait(chunk(got_zq, 0, dx), r_zq.at[dx])
        out = chunk(fin.at[0], 0, dx)
        out[...] = add(chunk(dqa, 0, dx), chunk(got_c, 0, dx), chunk(got_zq, 0, dx))
        give(0, fin.at[0], tx * GROUP, tx, y * 4 + x, dx)
    for n, own in ((1, dkb), (2, dvb)):
        for i in range(3):
            wait(slab(bgot_x.at[n - 1], i), r_bx.at[n - 1, i])
        bfin[n] = add(slab(own, x), *[slab(bgot_x.at[n - 1], i) for i in range(3)])
        give(n, bfin.at[n], 0, x, 16 + y, 0)
    for i in range(3):
        wait(slab(bgot_z, i), r_bz.at[i])
    bfin[0] = add(slab(dqb, k * 4 + z), slab(bgot_c, z), *[slab(bgot_z, i) for i in range(3)])
    give(0, bfin.at[0], 0, x, 16 + y, 0)

    for n in range(3):
        wait(outs[n], r_out.at[n])
        wait(dqa.at[pl.ds(0, 18 * BLK), :], s_out.at[n])
    wait(dqa.at[pl.ds(0, 8 * GROUP), :], s_c)
    wait(dqa.at[pl.ds(0, 8 * GROUP), :], s_zk)
    wait(put_zq, s_zq)
    wait(bgot_c, s_bc)
    wait(bgot_z, s_bz)
    wait(dqa.at[pl.ds(0, 6 * GROUP), :], s_bx)


def body(queries, key_rows, value_rows, forward_out, out_grad, log_norm, block_order, pattern):
    wide = lambda n: jax.ShapeDtypeStruct((n * BLK, BLK), BF)
    aux = lambda n: jax.ShapeDtypeStruct((n, 8, BLK), F32)
    any_ = pl.BlockSpec(memory_space=HBM)
    vmem = pl.BlockSpec(memory_space=VMEM)
    smem = pl.BlockSpec(memory_space=pltpu.SMEM)
    sem = lambda *shape: pltpu.SemaphoreType.DMA(shape)
    one = pltpu.SemaphoreType.DMA
    tokens, width = queries.shape

    gathered = pl.pallas_call(
        gather_kernel,
        out_shape=(
            wide(64), wide(64), aux(64), wide(32), wide(32),
            wide(32), wide(32), aux(32), wide(16), wide(16),
            jax.ShapeDtypeStruct((BLK, BLK), jnp.int32),
        ),
        in_specs=[any_] * 5 + [vmem] * 3,
        out_specs=(any_,) * 10 + (vmem,),
        scratch_shapes=[
            VMEM((tokens, width), BF), VMEM((tokens, width), BF), VMEM((HEADS, 8, BLK), F32),
            VMEM((BLK, BLK), F32), VMEM((BLK, BLK), F32),
            sem(2), sem(5), sem(5, 4), sem(5), sem(5), sem(5), sem(5, 4), sem(5), sem(5), sem(5), sem(5), sem(2), sem(2),
            sem(5), sem(5, 4), sem(5), sem(5), sem(2), sem(2),
        ],
        compiler_params=pltpu.CompilerParams(
            collective_id=0, has_side_effects=True, vmem_limit_bytes=16 * 2**20
        ),
        name="gather_blocks",
    )(
        queries, key_rows, value_rows, out_grad, forward_out, log_norm, pattern,
        block_order.reshape(1, BLK),
    )
    table = gathered[-1]

    grads = pl.pallas_call(
        compute_kernel,
        out_shape=(wide(64), wide(32), wide(32), wide(32), wide(16), wide(16)),
        in_specs=[smem] + [vmem] * 10,
        out_specs=(vmem,) * 6,
        scratch_shapes=[VMEM((32 * BLK, BLK), F32), VMEM((32 * BLK, BLK), F32), VMEM((GROUP, BLK), F32)],
        compiler_params=pltpu.CompilerParams(vmem_limit_bytes=56 * 2**20),
        name="block_grads",
    )(table, *gathered[:10])

    flat = jax.ShapeDtypeStruct((tokens, width), BF)
    return pl.pallas_call(
        return_kernel,
        out_shape=(flat, flat, flat),
        in_specs=[vmem] * 6,
        out_specs=(any_,) * 3,
        scratch_shapes=[
            VMEM((2, 16 * BLK, BLK), BF), VMEM((32 * BLK, BLK), BF), VMEM((16 * BLK, BLK), BF),
            VMEM((16 * BLK, BLK), BF), VMEM((3, 16 * BLK, BLK), BF),
            VMEM((16 * BLK, BLK), BF), VMEM((16 * BLK, BLK), BF), VMEM((12 * BLK, BLK), BF),
            VMEM((2, 12 * BLK, BLK), BF), VMEM((3, GROUP, BLK), BF),
            one, sem(2, 4), one, sem(2, 4), one, sem(4), one, one, one, sem(3), one, sem(2, 3), sem(3), sem(3),
        ],
        compiler_params=pltpu.CompilerParams(
            collective_id=1, has_side_effects=True, vmem_limit_bytes=40 * 2**20
        ),
        name="return_grads",
    )(*grads)


def solution(mesh):
    tokens = P(("ctx", "head"), None)
    return jax.shard_map(
        body,
        mesh=mesh,
        in_specs=(tokens,) * 6 + (P(), P()),
        out_specs=(tokens,) * 3,
        check_vma=False,
    )
```

```python
import functools

import jax
import jax.numpy as jnp
from jax import lax
from jax.experimental import pallas as pl
from jax.experimental.pallas import tpu as pltpu
from jax.sharding import PartitionSpec as P

MESH = pl.DeviceIdType.MESH
HBM = pl.ANY
VMEM = pltpu.VMEM
BF = jnp.bfloat16
F32 = jnp.float32
BLK = 128
HEADS = 20
LOG2E = 1.4426950408889634
SCALE = 128 ** -0.5
FAR = 1e30
GROUP = 4 * BLK
VMEM_LIMIT = 60 * 2**20


def coords():
    c = lax.axis_index("ctx")
    return c // 8, (c // 2) % 4, c % 2, lax.axis_index("head")


def dev(x, z, k, y):
    return (x * 8 + z * 2 + k, y)


def rows(start, size):
    return pl.ds(pl.multiple_of(start, BLK), size)


def cols(head):
    return pl.ds(pl.multiple_of(head * BLK, BLK), BLK)


def q_pair(z):
    return z + 1 - 2 * (z % 2)


def k_pair(z):
    return (z + 3 + 2 * (z % 2)) % 4


def send(src, dst, ss, rs, to):
    pltpu.make_async_remote_copy(
        src_ref=src, dst_ref=dst, send_sem=ss, recv_sem=rs, device_id=to, device_id_type=MESH
    ).start()


def wait(ref, sem):
    pltpu.make_async_copy(ref, ref, sem).wait()


def greet():
    x, z, k, y = coords()
    barrier = pltpu.get_barrier_semaphore()
    peers = [dev((x + dx) % 4, z, k, (y + dy) % 4) for dx in range(4) for dy in range(4) if dx or dy]
    peers += [dev(x, (z + dz) % 4, k, y) for dz in range(1, 4)]
    peers.append(dev(x, z, 1 - k, y))
    for peer in peers:
        pl.semaphore_signal(barrier, inc=1, device_id=peer, device_id_type=MESH)
    pl.semaphore_wait(barrier, len(peers))


DX = (0, 1, 3, 2)
AHEAD = 6
BSTEP = 3


def gather_kernel(
    q_in, k_in, v_in, g_in, o_in, norm_in, pat_in, order_in,
    qa, ga, xa, ka, va, qb, gb, xb, kb, vb, table,
    g_v, o_v, aux, pat_v,
    load_sem, sa1, ra1, sb1, rb1, s_zq, r_zq, s_c, r_c, s_c2, r_c2, s_zk, r_zk,
    s_bz, r_bz, s_bc, r_bc, s_bx, r_bx,
):
    x, z, k, y = coords()
    load_g = pltpu.make_async_copy(g_in, g_v, load_sem.at[0])
    load_o = pltpu.make_async_copy(o_in, o_v, load_sem.at[1])
    load_g.start()
    load_o.start()
    greet()
    mine = (x * 4 + y) * BLK

    slot = k * 4 + z
    wide = {0: (q_in, qa, qb), 1: (g_in, ga, gb), 2: (k_in, ka, kb), 3: (v_in, va, vb), 4: (aux, xa, xb)}

    def cut(a, head):
        src = wide[a][0]
        return src.at[head] if a == 4 else src.at[:, cols(head)]

    def scatter_a(a, wave):
        dst = xa.at[x * 4 + y] if a == 4 else wide[a][1].at[rows(mine, BLK), :]
        for dx in range(4):
            dy = (dx + wave) % 4
            tx, ty = (x + dx) % 4, (y + dy) % 4
            src = cut(a, ty * 4 + tx)
            if dx or dy:
                send(src, dst, sa1.at[a], ra1.at[a, wave], dev(tx, z, k, ty))
            else:
                pltpu.make_async_copy(src, dst, ra1.at[a, wave]).start()

    def scatter_b(a):
        if a == 4:
            dst = xb.at[slot * 4 + y]
        else:
            dst = wide[a][2].at[rows((slot if a < 2 else x) * GROUP + y * BLK, BLK), :]
        for dy in range(4):
            ty = (y + dy) % 4
            if dy:
                send(cut(a, 16 + ty), dst, sb1.at[a], rb1.at[a], dev(x, z, k, ty))
            else:
                pltpu.make_async_copy(cut(a, 16 + ty), dst, rb1.at[a]).start()

    steps = [(a, wave) for wave in range(4) for a in (0, 2, 1, 3)]
    for a in (0, 2, 1, 3):
        scatter_b(a)
    for step in steps[:AHEAD]:
        scatter_a(*step)

    load_g.wait()
    load_o.wait()
    for h in range(HEADS):
        prod = g_v[:, h * BLK:(h + 1) * BLK].astype(F32) * o_v[:, h * BLK:(h + 1) * BLK].astype(F32)
        dot = jnp.sum(prod.T, axis=0, keepdims=True)
        aux[h] = jnp.concatenate([norm_in[h:h + 1] * LOG2E, dot, jnp.zeros((6, BLK), F32)], axis=0)

    for wave in range(4):
        scatter_a(4, wave)
    scatter_b(4)

    def part(a, ref, quad, wave, dx):
        at = (quad * 4 + (x + 4 - dx) % 4) * 4 + (y + 8 - dx - wave) % 4
        return ref.at[pl.ds(at, 1)] if a == 4 else ref.at[rows(at * BLK, BLK), :]

    def whole(a, ref, count=4):
        return ref.at[pl.ds(0, count)] if a == 4 else ref.at[pl.ds(0, count * BLK), :]

    buf_a = {0: qa, 1: ga, 2: ka, 3: va, 4: xa}
    buf_b = {0: qb, 1: gb, 2: kb, 3: vb, 4: xb}
    to_q = dev(x, q_pair(z), k, y)
    to_k = dev(x, k_pair(z), k, y)
    to_c = dev(x, z, 1 - k, y)

    def forward_a(a, wave):
        ref = buf_a[a]
        wait(whole(a, ref), ra1.at[a, wave])
        for dx in range(4):
            own, there = part(a, ref, 0, wave, dx), part(a, ref, 1, wave, dx)
            if a in (2, 3):
                send(own, there, s_zk.at[a - 2], r_zk.at[a - 2], to_k)
            else:
                send(own, there, s_zq.at[a], r_zq.at[a, wave], to_q)
                send(own, part(a, ref, 2, wave, dx), s_c.at[a], r_c.at[a], to_c)

    def slab(a, ref, index, count=1):
        if a == 4:
            return ref.at[pl.ds(index * 4, 4 * count)]
        return ref.at[rows(index * GROUP, GROUP * count), :]

    def forward_b():
        for a in (0, 1, 4):
            ref = buf_b[a]
            own = slab(a, ref, slot)
            wait(own, rb1.at[a])
            for dz in (1, 3, 2):
                send(own, own, s_bz.at[a], r_bz.at[a, dz], dev(x, (z + dz) % 4, k, y))
            send(own, own, s_bc.at[a], r_bc.at[a], to_c)
        for a in (2, 3):
            ref = buf_b[a]
            own = slab(a, ref, x)
            wait(own, rb1.at[a])
            for dx in (1, 3, 2):
                send(own, own, s_bx.at[a - 2], r_bx.at[a - 2], dev((x + dx) % 4, z, k, y))

    for n, step in enumerate(steps):
        if n == BSTEP:
            forward_b()
        forward_a(*step)
        if n + AHEAD < 16:
            scatter_a(*steps[n + AHEAD])
    for wave in range(4):
        forward_a(4, wave)

    pat_v[...] = jnp.full((BLK, BLK), -1.0, F32)
    pat_v[0:36, :] = pat_in[...].astype(F32)
    order = jnp.broadcast_to(order_in[...].astype(F32), (BLK, BLK))
    i0 = lax.broadcasted_iota(jnp.int32, (BLK, BLK), 0)
    i1 = lax.broadcasted_iota(jnp.int32, (BLK, BLK), 1)
    hot = jnp.where(i0.astype(F32) == order, 1.0, 0.0)
    pat_v[...] = jnp.dot(pat_v[...].astype(BF), hot.astype(BF), preferred_element_type=F32)
    order_t = order.T
    adj = jnp.zeros((BLK, BLK), F32)
    for e in range(36):
        adj = jnp.where(pat_v[e:e + 1, :] == order_t, 1.0, adj)
    adj = adj.T
    local = (i0 // 4) == (i1 // 4)
    pick = jnp.where((i0 // 4) == i1, (i0 % 4 + 1).astype(F32), 0.0)
    own_cols = jnp.where(i1 == 32 + i0 % 4, 1.0, 0.0)
    table[...] = (
        jnp.dot(jnp.where(local, 0.0, adj).astype(BF), pick.astype(BF), preferred_element_type=F32)
        + jnp.dot(jnp.where(local, adj, 0.0).astype(BF), own_cols.astype(BF), preferred_element_type=F32)
    ).astype(jnp.int32)

    for dz in (1, 3, 2):
        for a in (0, 1, 4):
            ref = buf_b[a]
            got = slab(a, ref, k * 4 + (z + 4 - dz) % 4)
            wait(got, r_bz.at[a, dz])
            send(got, got, s_bc.at[a], r_bc.at[a], to_c)
    for wave in range(4):
        for a in (0, 1, 4):
            ref = buf_a[a]
            wait(whole(a, ref), r_zq.at[a, wave])
            for dx in range(4):
                send(part(a, ref, 1, wave, dx), part(a, ref, 3, wave, dx), s_c2.at[a], r_c2.at[a], to_c)

    def quad(a, ref, index):
        if a == 4:
            return ref.at[pl.ds(index * 16, 16)]
        return ref.at[pl.ds(index * 4 * GROUP, 4 * GROUP), :]

    for a in (2, 3):
        wait(quad(a, buf_a[a], 1), r_zk.at[a - 2])
        wait(quad(a, buf_a[a], 0), s_zk.at[a - 2])
        wait(slab(a, buf_b[a], 0, 3), r_bx.at[a - 2])
        wait(slab(a, buf_b[a], 0, 3), s_bx.at[a - 2])
    for a in (0, 1, 4):
        wait(quad(a, buf_a[a], 2), r_c.at[a])
        wait(quad(a, buf_a[a], 3), r_c2.at[a])
        wait(quad(a, buf_a[a], 0), s_zq.at[a])
        wait(quad(a, buf_a[a], 0), s_c.at[a])
        wait(quad(a, buf_a[a], 0), s_c2.at[a])
        wait(slab(a, buf_b[a], 0, 4), r_bc.at[a])
        wait(slab(a, buf_b[a], 0, 4), s_bc.at[a])
        wait(slab(a, buf_b[a], 0, 3), s_bz.at[a])
    for a in range(5):
        ref = buf_a[a]
        if a == 4:
            wait(ref.at[pl.ds(0, 15)], sa1.at[a])
            wait(ref.at[pl.ds(0, 3)], sb1.at[a])
        else:
            wait(ref.at[pl.ds(0, 15 * BLK), :], sa1.at[a])
            wait(ref.at[pl.ds(0, 3 * BLK), :], sb1.at[a])


def compute_kernel(
    table, qa_in, ga_in, xa_in, ka_in, va_in, qb_in, gb_in, xb_in, kb_in, vb_in,
    dqa_out, dka_out, dva_out, dqb_out, dkb_out, dvb_out,
    qa, ga, xa, ka, va, qb, gb, xb, kb, vb, dqa, dka, dva, dqb, dkb, dvb, in_sem, out_sem,
    acc_k, acc_v, kt_ref, s_ref, d_ref, p_ref, e_ref,
):
    x, z, k, y = coords()
    base2 = SCALE * LOG2E
    zq, zk = q_pair(z), k_pair(z)
    pairs_in = [
        (ka_in, ka), (va_in, va), (qa_in, qa), (ga_in, ga), (xa_in, xa),
        (kb_in, kb), (vb_in, vb), (qb_in, qb), (gb_in, gb), (xb_in, xb),
    ]
    loads = [pltpu.make_async_copy(src, dst, in_sem.at[i]) for i, (src, dst) in enumerate(pairs_in)]
    for load in loads:
        load.start()
    stores = []

    def store(src, dst):
        copy = pltpu.make_async_copy(src, dst, out_sem.at[len(stores)])
        copy.start()
        stores.append(copy)

    def lanes(x_ref, q, row):
        return jnp.concatenate([x_ref[q * 4 + b, row:row + 1, :] for b in range(4)], axis=1)

    def blocks(ref, places, axis=0):
        return jnp.concatenate([ref[pl.ds(p, BLK), :] for p in places], axis=axis)

    def span(q):
        return pl.ds(pl.multiple_of(q * GROUP, GROUP), GROUP)

    def picked(c, groups):
        places, biases = [], []
        for first, key_index in groups:
            for i in range(4):
                code = table[4 * c, key_index(i)]
                places.append(pl.multiple_of((first + i) * GROUP + jnp.maximum(code - 1, 0) * BLK, BLK))
                biases.append(jnp.where(code > 0, 0.0, FAR))
        return places, biases

    def soften(score, dprob, norm, dot, hide=None):
        prob = jnp.exp2(score * base2 - norm)
        if hide is not None:
            prob = jnp.where(hide, 0.0, prob)
        return prob.astype(BF), (prob * (dprob - dot)).astype(BF)

    def stage_1(q_ref, g_ref, k_ref, v_ref, q, places, s, d):
        s[...] = jnp.dot(blocks(k_ref, places), q_ref[span(q), :].T, preferred_element_type=F32)
        d[...] = jnp.dot(blocks(v_ref, places), g_ref[span(q), :].T, preferred_element_type=F32)

    def stage_2(x_ref, q, biases, s, d, p, e):
        norm, dot = lanes(x_ref, q, 0), lanes(x_ref, q, 1)
        for i, bias in enumerate(biases):
            cut = slice(i * BLK, (i + 1) * BLK)
            p[cut, :], e[cut, :] = soften(s[cut, :], d[cut, :], norm + bias, dot)

    def stage_3(q_ref, g_ref, dq_ref, q, places, p, e):
        dk = jnp.dot(e[...], q_ref[span(q), :], preferred_element_type=F32)
        dv = jnp.dot(p[...], g_ref[span(q), :], preferred_element_type=F32)
        dq = jnp.dot(blocks(kt_ref, places, 1), e[...], preferred_element_type=F32)
        for i, at in enumerate(places):
            acc_k[pl.ds(at, BLK), :] += dk[i * BLK:(i + 1) * BLK]
            acc_v[pl.ds(at, BLK), :] += dv[i * BLK:(i + 1) * BLK]
        dq_ref[span(q), :] = (dq * SCALE).T.astype(BF)

    def turn(k_ref, n):
        def step(i, carry):
            at = pl.ds(pl.multiple_of(i * BLK, BLK), BLK)
            kt_ref[at, :] = k_ref[at, :].T
            return carry

        lax.fori_loop(0, n, step, 0)

    def finish(dk_ref, dv_ref, n):
        def step(i, carry):
            at = span(i)
            dk_ref[at, :] = (acc_k[at, :] * SCALE).astype(BF)
            dv_ref[at, :] = acc_v[at, :].astype(BF)
            acc_k[at, :] = jnp.zeros((GROUP, BLK), F32)
            acc_v[at, :] = jnp.zeros((GROUP, BLK), F32)
            return carry

        lax.fori_loop(0, n, step, 0)

    def main(q_ref, g_ref, x_ref, k_ref, v_ref, dq_ref, count, c_of, groups):
        n = len(groups) * GROUP
        s, d = s_ref.at[:, 0:n, :], d_ref.at[:, 0:n, :]
        p, e = p_ref.at[:, 0:n, :], e_ref.at[:, 0:n, :]

        def one(t, half, stages):
            now, then = half, 1 - half
            if 3 in stages:
                places3, _ = picked(c_of(t - 2), groups)
                stage_3(q_ref, g_ref, dq_ref, t - 2, places3, p.at[now], e.at[now])
            if 1 in stages:
                places1, _ = picked(c_of(t), groups)
                stage_1(q_ref, g_ref, k_ref, v_ref, t, places1, s.at[now], d.at[now])
            if 2 in stages:
                _, biases2 = picked(c_of(t - 1), groups)
                stage_2(x_ref, t - 1, biases2, s.at[then], d.at[then], p.at[then], e.at[then])

        def step(it, carry):
            for half in range(2):
                one(2 * it + half, half, (1, 2, 3))
            return carry

        one(0, 0, (1,))
        one(1, 1, (1, 2))
        lax.fori_loop(1, count // 2, step, 0)
        one(count, 0, (2, 3))
        one(count + 1, 1, (3,))

    def diag(q_ref, g_ref, x_ref, k_ref, v_ref, dq_ref, q, c, own):
        here = span(own)
        places = [pl.multiple_of(own * GROUP + b * BLK, BLK) for b in range(4)]
        query, grad = q_ref[span(q), :], g_ref[span(q), :]
        score = jnp.dot(k_ref[here, :], query.T, preferred_element_type=F32)
        dprob = jnp.dot(v_ref[here, :], grad.T, preferred_element_type=F32)
        norm, dot = lanes(x_ref, q, 0), lanes(x_ref, q, 1)
        probs, scores = [], []
        key_at = lax.broadcasted_iota(jnp.int32, (BLK, GROUP), 0)
        query_at = lax.broadcasted_iota(jnp.int32, (BLK, GROUP), 1)
        for i in range(4):
            bias = jnp.concatenate(
                [
                    jnp.full((1, BLK), jnp.where(table[4 * c + b, 32 + i] > 0, 0.0, FAR), F32)
                    for b in range(4)
                ],
                axis=1,
            )
            hide = (query_at >= i * BLK) & (query_at < key_at + i * BLK)
            cut = slice(i * BLK, (i + 1) * BLK)
            prob, score_e = soften(score[cut], dprob[cut], norm + bias, dot, hide)
            probs.append(prob)
            scores.append(score_e)
        prob = jnp.concatenate(probs, axis=0)
        score = jnp.concatenate(scores, axis=0)
        acc_k[here, :] += jnp.dot(score, query, preferred_element_type=F32)
        acc_v[here, :] += jnp.dot(prob, grad, preferred_element_type=F32)
        dq = jnp.dot(blocks(kt_ref, places, 1), score, preferred_element_type=F32)
        dq_ref[span(q), :] = (dq_ref[span(q), :].astype(F32) + (dq * SCALE).T).astype(BF)

    acc_k[...] = jnp.zeros_like(acc_k)
    acc_v[...] = jnp.zeros_like(acc_v)

    def index_a(q):
        quad, xq = q // 4, q % 4
        zc = jnp.where(quad % 2 == 0, z, zq)
        kc = jnp.where(quad < 2, k, 1 - k)
        return xq * 8 + zc * 2 + kc

    loads[0].wait()
    turn(ka, 32)
    for load in loads[1:5]:
        load.wait()
    main(qa, ga, xa, ka, va, dqa, 16, index_a, [(0, lambda i: i * 8 + z * 2 + k), (4, lambda i: i * 8 + zk * 2 + k)])

    late = pl.ds(4 * GROUP, 12 * GROUP)
    store(dqa.at[late, :], dqa_out.at[late, :])

    def diag_a(q, carry):
        diag(qa, ga, xa, ka, va, dqa, q, index_a(q), q)
        return carry

    lax.fori_loop(0, 4, diag_a, 0)
    early = pl.ds(0, 4 * GROUP)
    store(dqa.at[early, :], dqa_out.at[early, :])
    finish(dka, dva, 8)
    store(dka, dka_out)
    store(dva, dva_out)
    for load in loads[5:]:
        load.wait()

    turn(kb, 16)
    main(qb, gb, xb, kb, vb, dqb, 8, lambda q: x * 8 + (q % 4) * 2 + q // 4, [(0, lambda i: i * 8 + z * 2 + k)])
    diag(qb, gb, xb, kb, vb, dqb, k * 4 + z, x * 8 + z * 2 + k, x)
    store(dqb, dqb_out)
    finish(dkb, dvb, 4)
    store(dkb, dkb_out)
    store(dvb, dvb_out)
    for copy in stores:
        copy.wait()


def compute_call(table, *gathered):
    wide = lambda n: jax.ShapeDtypeStruct((n * BLK, BLK), BF)
    any_ = pl.BlockSpec(memory_space=HBM)
    hold = lambda n: VMEM((n * BLK, BLK), BF)
    aux = lambda n: VMEM((n, 8, BLK), F32)
    return pl.pallas_call(
        compute_kernel,
        out_shape=(wide(64), wide(32), wide(32), wide(32), wide(16), wide(16)),
        in_specs=[pl.BlockSpec(memory_space=pltpu.SMEM)] + [any_] * 10,
        out_specs=(any_,) * 6,
        scratch_shapes=[
            hold(64), hold(64), aux(64), hold(32), hold(32), hold(32), hold(32), aux(32), hold(16), hold(16),
            hold(64), hold(32), hold(32), hold(32), hold(16), hold(16),
            pltpu.SemaphoreType.DMA((10,)), pltpu.SemaphoreType.DMA((7,)),
            VMEM((32 * BLK, BLK), F32), VMEM((32 * BLK, BLK), F32), hold(32),
            VMEM((2, 8 * BLK, GROUP), F32), VMEM((2, 8 * BLK, GROUP), F32),
            VMEM((2, 8 * BLK, GROUP), BF), VMEM((2, 8 * BLK, GROUP), BF),
        ],
        compiler_params=pltpu.CompilerParams(vmem_limit_bytes=VMEM_LIMIT),
        name="block_grads",
    )(table, *gathered)


def return_kernel(
    dqa, dka, dva, dqb, dkb, dvb,
    dq_out, dk_out, dv_out,
    own_q, own_k, own_v, own_bq, own_bk, own_bv, own_sem,
    got_zk, got_c, got_zq, put_zq, fin, bgot_c, bput_q, bgot_z, bgot_x, bfin,
    s_zk, r_zk, s_c, r_c, s_zq, r_zq, s_bc, r_bc, s_bz, r_bz, s_bx, r_bx, s_out, r_out,
):
    x, z, k, y = coords()
    outs = (dq_out, dk_out, dv_out)
    to_q = dev(x, q_pair(z), k, y)
    to_k = dev(x, k_pair(z), k, y)
    to_c = dev(x, z, 1 - k, y)
    half, quarter = pl.ds(0, 4 * GROUP), rows(x * GROUP, GROUP)
    loads = [
        pltpu.make_async_copy(src, dst, own_sem.at[i])
        for i, (src, dst) in enumerate([
            (dqa.at[pl.ds(0, 8 * GROUP), :], own_q),
            (dqb.at[rows(k * 4 * GROUP, 4 * GROUP), :], own_bq),
            (dka.at[half, :], own_k), (dva.at[half, :], own_v),
            (dkb.at[quarter, :], own_bk), (dvb.at[quarter, :], own_bv),
        ])
    ]
    for load in loads:
        load.start()
    greet()

    def chunk(ref, quad, dx):
        return ref.at[rows((quad * 4 + (x + dx) % 4) * GROUP, GROUP), :]

    def slab(ref, index):
        return ref.at[rows(index * GROUP, GROUP), :]

    for dx in DX:
        send(chunk(dqa, 3, dx), chunk(got_c, 1, dx), s_c, r_c.at[1, dx], to_c)
    send(dqb.at[rows((1 - k) * 4 * GROUP, 4 * GROUP), :], bgot_c, s_bc, r_bc, to_c)
    for dx in DX:
        for n, src in enumerate((dka, dva)):
            send(chunk(src, 1, dx), chunk(got_zk.at[n], 0, dx), s_zk, r_zk.at[n, dx], to_k)
    for dx in DX:
        send(chunk(dqa, 2, dx), chunk(got_c, 0, dx), s_c, r_c.at[0, dx], to_c)
    for dx in (1, 3, 2):
        for n, src in enumerate((dkb, dvb)):
            send(slab(src, (x + dx) % 4), slab(bgot_x.at[n], dx - 1), s_bx, r_bx.at[n, dx - 1], dev((x + dx) % 4, z, k, y))

    def add(*refs):
        total = refs[0][...].astype(F32)
        for ref in refs[1:]:
            total = total + ref[...].astype(F32)
        return total.astype(BF)

    for load in loads:
        load.wait()

    for dx in DX:
        wait(chunk(got_c, 1, dx), r_c.at[1, dx])
        part = chunk(put_zq, 0, dx)
        part[...] = add(chunk(own_q, 1, dx), chunk(got_c, 1, dx))
        send(part, chunk(got_zq, 0, dx), s_zq, r_zq.at[dx], to_q)
    wait(bgot_c, r_bc)
    for dz in (1, 3, 2):
        zt = (z + dz) % 4
        part = slab(bput_q, zt)
        part[...] = add(slab(own_bq, zt), slab(bgot_c, zt))
        send(part, slab(bgot_z, dz - 1), s_bz, r_bz.at[dz - 1], dev(x, zt, k, y))

    def give(n, src, base, tx, head_of, dx):
        for dy in range(4):
            ty = (y + dy) % 4
            block = src.at[rows(base + ty * BLK, BLK), :]
            dst = outs[n].at[:, cols(head_of)]
            if dx or dy:
                send(block, dst, s_out.at[n], r_out.at[n], dev(tx, z, k, ty))
            else:
                pltpu.make_async_copy(block, dst, r_out.at[n]).start()

    for dx in (1, 3, 2, 0):
        tx = (x + dx) % 4
        for n, own in ((1, own_k), (2, own_v)):
            wait(chunk(got_zk.at[n - 1], 0, dx), r_zk.at[n - 1, dx])
            out = chunk(fin.at[n], 0, dx)
            out[...] = add(chunk(own, 0, dx), chunk(got_zk.at[n - 1], 0, dx))
            give(n, fin.at[n], tx * GROUP, tx, y * 4 + x, dx)
    for dx in (1, 3, 2, 0):
        tx = (x + dx) % 4
        wait(chunk(got_c, 0, dx), r_c.at[0, dx])
        wait(chunk(got_zq, 0, dx), r_zq.at[dx])
        out = chunk(fin.at[0], 0, dx)
        out[...] = add(chunk(own_q, 0, dx), chunk(got_c, 0, dx), chunk(got_zq, 0, dx))
        give(0, fin.at[0], tx * GROUP, tx, y * 4 + x, dx)
    for n, own in ((1, own_bk), (2, own_bv)):
        for i in range(3):
            wait(slab(bgot_x.at[n - 1], i), r_bx.at[n - 1, i])
        bfin[n] = add(own, *[slab(bgot_x.at[n - 1], i) for i in range(3)])
        give(n, bfin.at[n], 0, x, 16 + y, 0)
    for i in range(3):
        wait(slab(bgot_z, i), r_bz.at[i])
    bfin[0] = add(slab(own_bq, z), slab(bgot_c, z), *[slab(bgot_z, i) for i in range(3)])
    give(0, bfin.at[0], 0, x, 16 + y, 0)

    for n in range(3):
        wait(outs[n], r_out.at[n])
        wait(dqa.at[pl.ds(0, 18 * BLK), :], s_out.at[n])
    wait(dqa.at[pl.ds(0, 8 * GROUP), :], s_c)
    wait(dqa.at[pl.ds(0, 8 * GROUP), :], s_zk)
    wait(put_zq, s_zq)
    wait(bgot_c, s_bc)
    wait(bgot_z, s_bz)
    wait(dqa.at[pl.ds(0, 6 * GROUP), :], s_bx)


def body(queries, key_rows, value_rows, forward_out, out_grad, log_norm, block_order, pattern):
    wide = lambda n: jax.ShapeDtypeStruct((n * BLK, BLK), BF)
    aux = lambda n: jax.ShapeDtypeStruct((n, 8, BLK), F32)
    any_ = pl.BlockSpec(memory_space=HBM)
    vmem = pl.BlockSpec(memory_space=VMEM)
    sem = lambda *shape: pltpu.SemaphoreType.DMA(shape)
    one = pltpu.SemaphoreType.DMA
    hold = lambda n: VMEM((n * BLK, BLK), BF)
    tokens, width = queries.shape

    gathered = pl.pallas_call(
        gather_kernel,
        out_shape=(
            wide(64), wide(64), aux(64), wide(32), wide(32),
            wide(32), wide(32), aux(32), wide(16), wide(16),
            jax.ShapeDtypeStruct((BLK, BLK), jnp.int32),
        ),
        in_specs=[any_] * 5 + [vmem] * 3,
        out_specs=(any_,) * 10 + (vmem,),
        scratch_shapes=[
            VMEM((tokens, width), BF), VMEM((tokens, width), BF), VMEM((HEADS, 8, BLK), F32),
            VMEM((BLK, BLK), F32),
            sem(2), sem(5), sem(5, 4), sem(5), sem(5), sem(5), sem(5, 4), sem(5), sem(5), sem(5), sem(5), sem(2), sem(2),
            sem(5), sem(5, 4), sem(5), sem(5), sem(2), sem(2),
        ],
        compiler_params=pltpu.CompilerParams(
            collective_id=0, has_side_effects=True, vmem_limit_bytes=VMEM_LIMIT
        ),
        name="gather_blocks",
    )(
        queries, key_rows, value_rows, out_grad, forward_out, log_norm.T, pattern.T,
        block_order.reshape(1, BLK),
    )
    table = gathered[-1]

    grads = compute_call(table, *gathered[:10])
    flat = jax.ShapeDtypeStruct((tokens, width), BF)
    return pl.pallas_call(
        return_kernel,
        out_shape=(flat, flat, flat),
        in_specs=[any_] * 6,
        out_specs=(any_,) * 3,
        scratch_shapes=[
            hold(32), hold(16), hold(16), hold(16), hold(4), hold(4), sem(6),
            VMEM((2, 16 * BLK, BLK), BF), VMEM((32 * BLK, BLK), BF), VMEM((16 * BLK, BLK), BF),
            VMEM((16 * BLK, BLK), BF), VMEM((3, 16 * BLK, BLK), BF),
            VMEM((16 * BLK, BLK), BF), VMEM((16 * BLK, BLK), BF), VMEM((12 * BLK, BLK), BF),
            VMEM((2, 12 * BLK, BLK), BF), VMEM((3, GROUP, BLK), BF),
            one, sem(2, 4), one, sem(2, 4), one, sem(4), one, one, one, sem(3), one, sem(2, 3), sem(3), sem(3),
        ],
        compiler_params=pltpu.CompilerParams(
            collective_id=1, has_side_effects=True, vmem_limit_bytes=VMEM_LIMIT
        ),
        name="return_grads",
    )(*grads)


def solution(mesh):
    tokens = P(("ctx", "head"), None)
    return jax.shard_map(
        body,
        mesh=mesh,
        in_specs=(tokens,) * 6 + (P(), P()),
        out_specs=(tokens,) * 3,
        check_vma=False,
    )
```

```python
import functools

import jax
import jax.numpy as jnp
from jax import lax
from jax.experimental import pallas as pl
from jax.experimental.pallas import tpu as pltpu
from jax.sharding import PartitionSpec as P

MESH = pl.DeviceIdType.MESH
HBM = pl.ANY
VMEM = pltpu.VMEM
BF = jnp.bfloat16
F32 = jnp.float32
BLK = 128
HEADS = 20
LOG2E = 1.4426950408889634
SCALE = 128 ** -0.5
FAR = 1e30
GROUP = 4 * BLK
VMEM_LIMIT = 60 * 2**20


def coords():
    c = lax.axis_index("ctx")
    return c // 8, (c // 2) % 4, c % 2, lax.axis_index("head")


def dev(x, z, k, y):
    return (x * 8 + z * 2 + k, y)


def rows(start, size):
    return pl.ds(pl.multiple_of(start, BLK), size)


def cols(head):
    return pl.ds(pl.multiple_of(head * BLK, BLK), BLK)


def q_pair(z):
    return z + 1 - 2 * (z % 2)


def k_pair(z):
    return (z + 3 + 2 * (z % 2)) % 4


def send(src, dst, ss, rs, to):
    pltpu.make_async_remote_copy(
        src_ref=src, dst_ref=dst, send_sem=ss, recv_sem=rs, device_id=to, device_id_type=MESH
    ).start()


def wait(ref, sem):
    pltpu.make_async_copy(ref, ref, sem).wait()


def greet():
    x, z, k, y = coords()
    barrier = pltpu.get_barrier_semaphore()
    peers = [dev((x + dx) % 4, z, k, (y + dy) % 4) for dx in range(4) for dy in range(4) if dx or dy]
    peers += [dev(x, (z + dz) % 4, k, y) for dz in range(1, 4)]
    peers.append(dev(x, z, 1 - k, y))
    for peer in peers:
        pl.semaphore_signal(barrier, inc=1, device_id=peer, device_id_type=MESH)
    pl.semaphore_wait(barrier, len(peers))


AHEAD = 6
ORDER = (1, 3, 2, 0)
BSTEP = 3


def gather_kernel(
    q_in, k_in, v_in, g_in, o_in, norm_in, pat_in, order_in,
    qa, ga, xa, ka, va, qb, gb, xb, kb, vb, table,
    g_v, o_v, aux, pat_v,
    load_sem, sa1, ra1, sb1, rb1, s_zq, r_zq, s_c, r_c, s_c2, r_c2, s_zk, r_zk,
    s_bz, r_bz, s_bc, r_bc, s_bx, r_bx,
):
    x, z, k, y = coords()
    load_g = pltpu.make_async_copy(g_in, g_v, load_sem.at[0])
    load_o = pltpu.make_async_copy(o_in, o_v, load_sem.at[1])
    load_g.start()
    load_o.start()
    greet()
    mine = (x * 4 + y) * BLK

    slot = k * 4 + z
    wide = {0: (q_in, qa, qb), 1: (g_in, ga, gb), 2: (k_in, ka, kb), 3: (v_in, va, vb), 4: (aux, xa, xb)}

    def cut(a, head):
        src = wide[a][0]
        return src.at[head] if a == 4 else src.at[:, cols(head)]

    def scatter_a(a, wave):
        dst = xa.at[x * 4 + y] if a == 4 else wide[a][1].at[rows(mine, BLK), :]
        dx = wave
        for dy in (2, 1, 3, 0):
            tx, ty = (x + dx) % 4, (y + dy) % 4
            src = cut(a, ty * 4 + tx)
            if dx or dy:
                send(src, dst, sa1.at[a], ra1.at[a, wave], dev(tx, z, k, ty))
            else:
                pltpu.make_async_copy(src, dst, ra1.at[a, wave]).start()

    def scatter_b(a):
        if a == 4:
            dst = xb.at[slot * 4 + y]
        else:
            dst = wide[a][2].at[rows((slot if a < 2 else x) * GROUP + y * BLK, BLK), :]
        for dy in range(4):
            ty = (y + dy) % 4
            if dy:
                send(cut(a, 16 + ty), dst, sb1.at[a], rb1.at[a], dev(x, z, k, ty))
            else:
                pltpu.make_async_copy(cut(a, 16 + ty), dst, rb1.at[a]).start()

    steps = [(a, wave) for wave in (2, 1, 3, 0) for a in (0, 2, 1, 3)]
    for a in (0, 2, 1, 3):
        scatter_b(a)
    for step in steps[:AHEAD]:
        scatter_a(*step)

    load_g.wait()
    load_o.wait()
    for h in range(HEADS):
        prod = g_v[:, h * BLK:(h + 1) * BLK].astype(F32) * o_v[:, h * BLK:(h + 1) * BLK].astype(F32)
        dot = jnp.sum(prod.T, axis=0, keepdims=True)
        aux[h] = jnp.concatenate([norm_in[h:h + 1] * LOG2E, dot, jnp.zeros((6, BLK), F32)], axis=0)

    for wave in range(4):
        scatter_a(4, wave)
    scatter_b(4)

    def part(a, ref, quad, dx):
        at = quad * 4 + (x + 4 - dx) % 4
        return ref.at[pl.ds(at * 4, 4)] if a == 4 else ref.at[rows(at * GROUP, GROUP), :]

    def whole(a, ref, count=4):
        return ref.at[pl.ds(0, count)] if a == 4 else ref.at[pl.ds(0, count * BLK), :]

    buf_a = {0: qa, 1: ga, 2: ka, 3: va, 4: xa}
    buf_b = {0: qb, 1: gb, 2: kb, 3: vb, 4: xb}
    to_q = dev(x, q_pair(z), k, y)
    to_k = dev(x, k_pair(z), k, y)
    to_c = dev(x, z, 1 - k, y)

    def forward_a(a, dx):
        ref = buf_a[a]
        own, there = part(a, ref, 0, dx), part(a, ref, 1, dx)
        wait(own, ra1.at[a, dx])
        if a in (2, 3):
            send(own, there, s_zk.at[a - 2], r_zk.at[a - 2], to_k)
        else:
            send(own, there, s_zq.at[a], r_zq.at[a, dx], to_q)
            send(own, part(a, ref, 2, dx), s_c.at[a], r_c.at[a], to_c)

    def slab(a, ref, index, count=1):
        if a == 4:
            return ref.at[pl.ds(index * 4, 4 * count)]
        return ref.at[rows(index * GROUP, GROUP * count), :]

    def forward_b():
        for a in (0, 1, 4):
            ref = buf_b[a]
            own = slab(a, ref, slot)
            wait(own, rb1.at[a])
            for dz in (1, 3, 2):
                send(own, own, s_bz.at[a], r_bz.at[a, dz], dev(x, (z + dz) % 4, k, y))
            send(own, own, s_bc.at[a], r_bc.at[a], to_c)
        for a in (2, 3):
            ref = buf_b[a]
            own = slab(a, ref, x)
            wait(own, rb1.at[a])
            for dx in (1, 3, 2):
                send(own, own, s_bx.at[a - 2], r_bx.at[a - 2], dev((x + dx) % 4, z, k, y))

    for n, step in enumerate(steps):
        if n == BSTEP:
            forward_b()
        forward_a(*step)
        if n + AHEAD < 16:
            scatter_a(*steps[n + AHEAD])
    for wave in range(4):
        forward_a(4, wave)

    pat_v[...] = jnp.full((BLK, BLK), -1.0, F32)
    pat_v[0:36, :] = pat_in[...].astype(F32)
    order = jnp.broadcast_to(order_in[...].astype(F32), (BLK, BLK))
    i0 = lax.broadcasted_iota(jnp.int32, (BLK, BLK), 0)
    i1 = lax.broadcasted_iota(jnp.int32, (BLK, BLK), 1)
    hot = jnp.where(i0.astype(F32) == order, 1.0, 0.0)
    pat_v[...] = jnp.dot(pat_v[...].astype(BF), hot.astype(BF), preferred_element_type=F32)
    order_t = order.T
    adj = jnp.zeros((BLK, BLK), F32)
    for e in range(36):
        adj = jnp.where(pat_v[e:e + 1, :] == order_t, 1.0, adj)
    adj = adj.T
    local = (i0 // 4) == (i1 // 4)
    pick = jnp.where((i0 // 4) == i1, (i0 % 4 + 1).astype(F32), 0.0)
    own_cols = jnp.where(i1 == 32 + i0 % 4, 1.0, 0.0)
    table[...] = (
        jnp.dot(jnp.where(local, 0.0, adj).astype(BF), pick.astype(BF), preferred_element_type=F32)
        + jnp.dot(jnp.where(local, adj, 0.0).astype(BF), own_cols.astype(BF), preferred_element_type=F32)
    ).astype(jnp.int32)

    for dz in (1, 3, 2):
        for a in (0, 1, 4):
            ref = buf_b[a]
            got = slab(a, ref, k * 4 + (z + 4 - dz) % 4)
            wait(got, r_bz.at[a, dz])
            send(got, got, s_bc.at[a], r_bc.at[a], to_c)
    for wave in (2, 1, 3, 0):
        for a in (0, 1, 4):
            ref = buf_a[a]
            wait(part(a, ref, 1, wave), r_zq.at[a, wave])
            send(part(a, ref, 1, wave), part(a, ref, 3, wave), s_c2.at[a], r_c2.at[a], to_c)

    def quad(a, ref, index):
        if a == 4:
            return ref.at[pl.ds(index * 16, 16)]
        return ref.at[pl.ds(index * 4 * GROUP, 4 * GROUP), :]

    for a in (2, 3):
        wait(quad(a, buf_a[a], 1), r_zk.at[a - 2])
        wait(quad(a, buf_a[a], 0), s_zk.at[a - 2])
        wait(slab(a, buf_b[a], 0, 3), r_bx.at[a - 2])
        wait(slab(a, buf_b[a], 0, 3), s_bx.at[a - 2])
    for a in (0, 1, 4):
        wait(quad(a, buf_a[a], 2), r_c.at[a])
        wait(quad(a, buf_a[a], 3), r_c2.at[a])
        wait(quad(a, buf_a[a], 0), s_zq.at[a])
        wait(quad(a, buf_a[a], 0), s_c.at[a])
        wait(quad(a, buf_a[a], 0), s_c2.at[a])
        wait(slab(a, buf_b[a], 0, 4), r_bc.at[a])
        wait(slab(a, buf_b[a], 0, 4), s_bc.at[a])
        wait(slab(a, buf_b[a], 0, 3), s_bz.at[a])
    for a in range(5):
        ref = buf_a[a]
        if a == 4:
            wait(ref.at[pl.ds(0, 15)], sa1.at[a])
            wait(ref.at[pl.ds(0, 3)], sb1.at[a])
        else:
            wait(ref.at[pl.ds(0, 15 * BLK), :], sa1.at[a])
            wait(ref.at[pl.ds(0, 3 * BLK), :], sb1.at[a])


def compute_kernel(
    table, qa_in, ga_in, xa_in, ka_in, va_in, qb_in, gb_in, xb_in, kb_in, vb_in,
    dqa_out, dka_out, dva_out, dqb_out, dkb_out, dvb_out,
    qa, ga, xa, ka, va, qb, gb, xb, kb, vb, dqa, dka, dva, dqb, dkb, dvb, in_sem, out_sem,
    acc_k, acc_v, kt_ref, s_ref, d_ref, p_ref, e_ref,
):
    x, z, k, y = coords()
    base2 = SCALE * LOG2E
    zq, zk = q_pair(z), k_pair(z)
    pairs_in = [
        (ka_in, ka), (va_in, va), (qa_in, qa), (ga_in, ga), (xa_in, xa),
        (kb_in, kb), (vb_in, vb), (qb_in, qb), (gb_in, gb), (xb_in, xb),
    ]
    loads = [pltpu.make_async_copy(src, dst, in_sem.at[i]) for i, (src, dst) in enumerate(pairs_in)]
    for load in loads:
        load.start()
    stores = []

    def store(src, dst):
        copy = pltpu.make_async_copy(src, dst, out_sem.at[len(stores)])
        copy.start()
        stores.append(copy)

    def lanes(x_ref, q, row):
        return jnp.concatenate([x_ref[q * 4 + b, row:row + 1, :] for b in range(4)], axis=1)

    def blocks(ref, places, axis=0):
        return jnp.concatenate([ref[pl.ds(p, BLK), :] for p in places], axis=axis)

    def span(q):
        return pl.ds(pl.multiple_of(q * GROUP, GROUP), GROUP)

    def picked(c, groups):
        places, biases = [], []
        for first, key_index in groups:
            for i in range(4):
                code = table[4 * c, key_index(i)]
                places.append(pl.multiple_of((first + i) * GROUP + jnp.maximum(code - 1, 0) * BLK, BLK))
                biases.append(jnp.where(code > 0, 0.0, FAR))
        return places, biases

    def soften(score, dprob, norm, dot, hide=None):
        prob = jnp.exp2(score * base2 - norm)
        if hide is not None:
            prob = jnp.where(hide, 0.0, prob)
        return prob.astype(BF), (prob * (dprob - dot)).astype(BF)

    def stage_1(q_ref, g_ref, k_ref, v_ref, q, places, s, d):
        s[...] = jnp.dot(blocks(k_ref, places), q_ref[span(q), :].T, preferred_element_type=F32)
        d[...] = jnp.dot(blocks(v_ref, places), g_ref[span(q), :].T, preferred_element_type=F32)

    def stage_2(x_ref, q, biases, s, d, p, e):
        norm, dot = lanes(x_ref, q, 0), lanes(x_ref, q, 1)
        for i, bias in enumerate(biases):
            cut = slice(i * BLK, (i + 1) * BLK)
            p[cut, :], e[cut, :] = soften(s[cut, :], d[cut, :], norm + bias, dot)

    def stage_3(q_ref, g_ref, dq_ref, q, places, p, e):
        dk = jnp.dot(e[...], q_ref[span(q), :], preferred_element_type=F32)
        dv = jnp.dot(p[...], g_ref[span(q), :], preferred_element_type=F32)
        dq = jnp.dot(blocks(kt_ref, places, 1), e[...], preferred_element_type=F32)
        for i, at in enumerate(places):
            acc_k[pl.ds(at, BLK), :] += dk[i * BLK:(i + 1) * BLK]
            acc_v[pl.ds(at, BLK), :] += dv[i * BLK:(i + 1) * BLK]
        dq_ref[span(q), :] = (dq * SCALE).T.astype(BF)

    def turn(k_ref, n):
        def step(i, carry):
            turned = k_ref[span(i), :].T
            for b in range(4):
                kt_ref[rows(i * GROUP + b * BLK, BLK), :] = turned[:, b * BLK:(b + 1) * BLK]
            return carry

        lax.fori_loop(0, n // 4, step, 0)

    def finish(dk_ref, dv_ref, n):
        def step(i, carry):
            at = span(i)
            dk_ref[at, :] = (acc_k[at, :] * SCALE).astype(BF)
            dv_ref[at, :] = acc_v[at, :].astype(BF)
            return carry

        lax.fori_loop(0, n, step, 0)

    def main(q_ref, g_ref, x_ref, k_ref, v_ref, dq_ref, count, c_of, groups):
        n = len(groups) * GROUP
        s, d = s_ref.at[:, 0:n, :], d_ref.at[:, 0:n, :]
        p, e = p_ref.at[:, 0:n, :], e_ref.at[:, 0:n, :]

        def one(t, half, stages):
            now, then = half, 1 - half
            if 3 in stages:
                places3, _ = picked(c_of(t - 2), groups)
                stage_3(q_ref, g_ref, dq_ref, t - 2, places3, p.at[now], e.at[now])
            if 1 in stages:
                places1, _ = picked(c_of(t), groups)
                stage_1(q_ref, g_ref, k_ref, v_ref, t, places1, s.at[now], d.at[now])
            if 2 in stages:
                _, biases2 = picked(c_of(t - 1), groups)
                stage_2(x_ref, t - 1, biases2, s.at[then], d.at[then], p.at[then], e.at[then])

        def step(it, carry):
            for half in range(2):
                one(2 * it + half, half, (1, 2, 3))
            return carry

        one(0, 0, (1,))
        one(1, 1, (1, 2))
        lax.fori_loop(1, count // 2, step, 0)
        one(count, 0, (2, 3))
        one(count + 1, 1, (3,))

    def diag(q_ref, g_ref, x_ref, k_ref, v_ref, dq_ref, q, c, own):
        here = span(own)
        places = [pl.multiple_of(own * GROUP + b * BLK, BLK) for b in range(4)]
        query, grad = q_ref[span(q), :], g_ref[span(q), :]
        score = jnp.dot(k_ref[here, :], query.T, preferred_element_type=F32)
        dprob = jnp.dot(v_ref[here, :], grad.T, preferred_element_type=F32)
        norm, dot = lanes(x_ref, q, 0), lanes(x_ref, q, 1)
        probs, scores = [], []
        key_at = lax.broadcasted_iota(jnp.int32, (BLK, GROUP), 0)
        query_at = lax.broadcasted_iota(jnp.int32, (BLK, GROUP), 1)
        for i in range(4):
            bias = jnp.concatenate(
                [
                    jnp.full((1, BLK), jnp.where(table[4 * c + b, 32 + i] > 0, 0.0, FAR), F32)
                    for b in range(4)
                ],
                axis=1,
            )
            hide = (query_at >= i * BLK) & (query_at < key_at + i * BLK)
            cut = slice(i * BLK, (i + 1) * BLK)
            prob, score_e = soften(score[cut], dprob[cut], norm + bias, dot, hide)
            probs.append(prob)
            scores.append(score_e)
        prob = jnp.concatenate(probs, axis=0)
        score = jnp.concatenate(scores, axis=0)
        acc_k[here, :] += jnp.dot(score, query, preferred_element_type=F32)
        acc_v[here, :] += jnp.dot(prob, grad, preferred_element_type=F32)
        dq = jnp.dot(blocks(kt_ref, places, 1), score, preferred_element_type=F32)
        dq_ref[span(q), :] = (dq_ref[span(q), :].astype(F32) + (dq * SCALE).T).astype(BF)

    acc_k[...] = jnp.zeros_like(acc_k)
    acc_v[...] = jnp.zeros_like(acc_v)

    def index_a(q):
        quad, xq = q // 4, q % 4
        zc = jnp.where(quad % 2 == 0, z, zq)
        kc = jnp.where(quad < 2, k, 1 - k)
        return xq * 8 + zc * 2 + kc

    loads[0].wait()
    turn(ka, 32)
    for load in loads[1:5]:
        load.wait()
    main(qa, ga, xa, ka, va, dqa, 16, index_a, [(0, lambda i: i * 8 + z * 2 + k), (4, lambda i: i * 8 + zk * 2 + k)])

    late = pl.ds(4 * GROUP, 12 * GROUP)
    store(dqa.at[late, :], dqa_out.at[late, :])

    for q in range(4):
        diag(qa, ga, xa, ka, va, dqa, q, index_a(q), q)
    early = pl.ds(0, 4 * GROUP)
    store(dqa.at[early, :], dqa_out.at[early, :])
    finish(dka, dva, 8)
    store(dka, dka_out)
    store(dva, dva_out)
    for load in loads[5:]:
        load.wait()

    acc_k[0:16 * BLK, :] = jnp.zeros((16 * BLK, BLK), F32)
    acc_v[0:16 * BLK, :] = jnp.zeros((16 * BLK, BLK), F32)
    turn(kb, 16)
    main(qb, gb, xb, kb, vb, dqb, 8, lambda q: x * 8 + (q % 4) * 2 + q // 4, [(0, lambda i: i * 8 + z * 2 + k)])
    diag(qb, gb, xb, kb, vb, dqb, k * 4 + z, x * 8 + z * 2 + k, x)
    store(dqb, dqb_out)
    finish(dkb, dvb, 4)
    store(dkb, dkb_out)
    store(dvb, dvb_out)
    for copy in stores:
        copy.wait()


def compute_call(table, *gathered):
    wide = lambda n: jax.ShapeDtypeStruct((n * BLK, BLK), BF)
    any_ = pl.BlockSpec(memory_space=HBM)
    hold = lambda n: VMEM((n * BLK, BLK), BF)
    aux = lambda n: VMEM((n, 8, BLK), F32)
    return pl.pallas_call(
        compute_kernel,
        out_shape=(wide(64), wide(32), wide(32), wide(32), wide(16), wide(16)),
        in_specs=[pl.BlockSpec(memory_space=pltpu.SMEM)] + [any_] * 10,
        out_specs=(any_,) * 6,
        scratch_shapes=[
            hold(64), hold(64), aux(64), hold(32), hold(32), hold(32), hold(32), aux(32), hold(16), hold(16),
            hold(64), hold(32), hold(32), hold(32), hold(16), hold(16),
            pltpu.SemaphoreType.DMA((10,)), pltpu.SemaphoreType.DMA((7,)),
            VMEM((32 * BLK, BLK), F32), VMEM((32 * BLK, BLK), F32), hold(32),
            VMEM((2, 8 * BLK, GROUP), F32), VMEM((2, 8 * BLK, GROUP), F32),
            VMEM((2, 8 * BLK, GROUP), BF), VMEM((2, 8 * BLK, GROUP), BF),
        ],
        compiler_params=pltpu.CompilerParams(vmem_limit_bytes=VMEM_LIMIT),
        name="block_grads",
    )(table, *gathered)


def return_kernel(
    dqa, dka, dva, dqb, dkb, dvb,
    dq_out, dk_out, dv_out,
    own_q, own_k, own_v, own_bq, own_bk, own_bv, own_sem,
    got_zk, got_c, got_zq, put_zq, fin, bgot_c, bput_q, bgot_z, bgot_x, bfin,
    s_zk, r_zk, s_c, r_c, s_zq, r_zq, s_bc, r_bc, s_bz, r_bz, s_bx, r_bx, s_out, r_out,
):
    x, z, k, y = coords()
    outs = (dq_out, dk_out, dv_out)
    to_q = dev(x, q_pair(z), k, y)
    to_k = dev(x, k_pair(z), k, y)
    to_c = dev(x, z, 1 - k, y)
    half, quarter = pl.ds(0, 4 * GROUP), rows(x * GROUP, GROUP)
    loads = [
        pltpu.make_async_copy(src, dst, own_sem.at[i])
        for i, (src, dst) in enumerate([
            (dqa.at[pl.ds(0, 8 * GROUP), :], own_q),
            (dqb.at[rows(k * 4 * GROUP, 4 * GROUP), :], own_bq),
            (dka.at[half, :], own_k), (dva.at[half, :], own_v),
            (dkb.at[quarter, :], own_bk), (dvb.at[quarter, :], own_bv),
        ])
    ]
    for load in loads:
        load.start()
    greet()

    def chunk(ref, quad, dx):
        return ref.at[rows((quad * 4 + (x + dx) % 4) * GROUP, GROUP), :]

    def slab(ref, index):
        return ref.at[rows(index * GROUP, GROUP), :]

    def add(*refs):
        total = refs[0][...].astype(F32)
        for ref in refs[1:]:
            total = total + ref[...].astype(F32)
        return total.astype(BF)

    def give(n, src, base, tx, head_of, dx):
        for dy in range(4):
            ty = (y + dy) % 4
            block = src.at[rows(base + ty * BLK, BLK), :]
            dst = outs[n].at[:, cols(head_of)]
            if dx or dy:
                send(block, dst, s_out.at[n], r_out.at[n], dev(tx, z, k, ty))
            else:
                pltpu.make_async_copy(block, dst, r_out.at[n]).start()

    def keys_out(dx):
        for n, src in enumerate((dka, dva)):
            send(chunk(src, 1, dx), chunk(got_zk.at[n], 0, dx), s_zk, r_zk.at[n, dx], to_k)

    def far_keys_out(dx):
        for n, src in enumerate((dkb, dvb)):
            to = dev((x + dx) % 4, z, k, y)
            send(slab(src, (x + dx) % 4), slab(bgot_x.at[n], dx - 1), s_bx, r_bx.at[n, dx - 1], to)

    def queries_on(dx):
        wait(chunk(got_c, 1, dx), r_c.at[1, dx])
        part = chunk(put_zq, 0, dx)
        part[...] = add(chunk(own_q, 1, dx), chunk(got_c, 1, dx))
        send(part, chunk(got_zq, 0, dx), s_zq, r_zq.at[dx], to_q)

    def far_queries_on(dz):
        zt = (z + dz) % 4
        part = slab(bput_q, zt)
        part[...] = add(slab(own_bq, zt), slab(bgot_c, zt))
        send(part, slab(bgot_z, dz - 1), s_bz, r_bz.at[dz - 1], dev(x, zt, k, y))

    def keys_home(dx):
        tx = (x + dx) % 4
        for n, own in ((1, own_k), (2, own_v)):
            wait(chunk(got_zk.at[n - 1], 0, dx), r_zk.at[n - 1, dx])
            out = chunk(fin.at[n], 0, dx)
            out[...] = add(chunk(own, 0, dx), chunk(got_zk.at[n - 1], 0, dx))
            give(n, fin.at[n], tx * GROUP, tx, y * 4 + x, dx)

    def queries_home(dx):
        tx = (x + dx) % 4
        wait(chunk(got_c, 0, dx), r_c.at[0, dx])
        wait(chunk(got_zq, 0, dx), r_zq.at[dx])
        out = chunk(fin.at[0], 0, dx)
        out[...] = add(chunk(own_q, 0, dx), chunk(got_c, 0, dx), chunk(got_zq, 0, dx))
        give(0, fin.at[0], tx * GROUP, tx, y * 4 + x, dx)

    def far_keys_home():
        for n, own in ((1, own_bk), (2, own_bv)):
            for i in range(3):
                wait(slab(bgot_x.at[n - 1], i), r_bx.at[n - 1, i])
            bfin[n] = add(own, *[slab(bgot_x.at[n - 1], i) for i in range(3)])
            give(n, bfin.at[n], 0, x, 16 + y, 0)

    def far_queries_home():
        for i in range(3):
            wait(slab(bgot_z, i), r_bz.at[i])
        bfin[0] = add(slab(own_bq, z), slab(bgot_c, z), *[slab(bgot_z, i) for i in range(3)])
        give(0, bfin.at[0], 0, x, 16 + y, 0)

    first, second, third, last = ORDER
    for dx in ORDER:
        send(chunk(dqa, 3, dx), chunk(got_c, 1, dx), s_c, r_c.at[1, dx], to_c)
    send(dqb.at[rows((1 - k) * 4 * GROUP, 4 * GROUP), :], bgot_c, s_bc, r_bc, to_c)
    keys_out(first)
    far_keys_out(1)
    far_keys_out(3)
    for load in loads:
        load.wait()
    for dx in ORDER:
        send(chunk(dqa, 2, dx), chunk(got_c, 0, dx), s_c, r_c.at[0, dx], to_c)
    for dx in ORDER:
        queries_on(dx)
    far_keys_out(2)
    for dx in ORDER[1:]:
        keys_out(dx)
    wait(bgot_c, r_bc)
    for dz in (1, 3, 2):
        far_queries_on(dz)
    for dx in ORDER:
        queries_home(dx)
        keys_home(dx)
        if dx == 1:
            far_keys_home()
    far_queries_home()

    for n in range(3):
        wait(outs[n], r_out.at[n])
        wait(dqa.at[pl.ds(0, 18 * BLK), :], s_out.at[n])
    wait(dqa.at[pl.ds(0, 8 * GROUP), :], s_c)
    wait(dqa.at[pl.ds(0, 8 * GROUP), :], s_zk)
    wait(put_zq, s_zq)
    wait(bgot_c, s_bc)
    wait(bgot_z, s_bz)
    wait(dqa.at[pl.ds(0, 6 * GROUP), :], s_bx)


def body(queries, key_rows, value_rows, forward_out, out_grad, log_norm, block_order, pattern):
    wide = lambda n: jax.ShapeDtypeStruct((n * BLK, BLK), BF)
    aux = lambda n: jax.ShapeDtypeStruct((n, 8, BLK), F32)
    any_ = pl.BlockSpec(memory_space=HBM)
    vmem = pl.BlockSpec(memory_space=VMEM)
    sem = lambda *shape: pltpu.SemaphoreType.DMA(shape)
    one = pltpu.SemaphoreType.DMA
    hold = lambda n: VMEM((n * BLK, BLK), BF)
    tokens, width = queries.shape

    gathered = pl.pallas_call(
        gather_kernel,
        out_shape=(
            wide(64), wide(64), aux(64), wide(32), wide(32),
            wide(32), wide(32), aux(32), wide(16), wide(16),
            jax.ShapeDtypeStruct((BLK, BLK), jnp.int32),
        ),
        in_specs=[any_] * 5 + [vmem] * 3,
        out_specs=(any_,) * 10 + (vmem,),
        scratch_shapes=[
            VMEM((tokens, width), BF), VMEM((tokens, width), BF), VMEM((HEADS, 8, BLK), F32),
            VMEM((BLK, BLK), F32),
            sem(2), sem(5), sem(5, 4), sem(5), sem(5), sem(5), sem(5, 4), sem(5), sem(5), sem(5), sem(5), sem(2), sem(2),
            sem(5), sem(5, 4), sem(5), sem(5), sem(2), sem(2),
        ],
        compiler_params=pltpu.CompilerParams(
            collective_id=0, has_side_effects=True, vmem_limit_bytes=VMEM_LIMIT
        ),
        name="gather_blocks",
    )(
        queries, key_rows, value_rows, out_grad, forward_out, log_norm.T, pattern.T,
        block_order.reshape(1, BLK),
    )
    table = gathered[-1]

    grads = compute_call(table, *gathered[:10])
    flat = jax.ShapeDtypeStruct((tokens, width), BF)
    return pl.pallas_call(
        return_kernel,
        out_shape=(flat, flat, flat),
        in_specs=[any_] * 6,
        out_specs=(any_,) * 3,
        scratch_shapes=[
            hold(32), hold(16), hold(16), hold(16), hold(4), hold(4), sem(6),
            VMEM((2, 16 * BLK, BLK), BF), VMEM((32 * BLK, BLK), BF), VMEM((16 * BLK, BLK), BF),
            VMEM((16 * BLK, BLK), BF), VMEM((3, 16 * BLK, BLK), BF),
            VMEM((16 * BLK, BLK), BF), VMEM((16 * BLK, BLK), BF), VMEM((12 * BLK, BLK), BF),
            VMEM((2, 12 * BLK, BLK), BF), VMEM((3, GROUP, BLK), BF),
            one, sem(2, 4), one, sem(2, 4), one, sem(4), one, one, one, sem(3), one, sem(2, 3), sem(3), sem(3),
        ],
        compiler_params=pltpu.CompilerParams(
            collective_id=1, has_side_effects=True, vmem_limit_bytes=VMEM_LIMIT
        ),
        name="return_grads",
    )(*grads)


def solution(mesh):
    tokens = P(("ctx", "head"), None)
    return jax.shard_map(
        body,
        mesh=mesh,
        in_specs=(tokens,) * 6 + (P(), P()),
        out_specs=(tokens,) * 3,
        check_vma=False,
    )
```

```python
import functools

import jax
import jax.numpy as jnp
from jax import lax
from jax.experimental import pallas as pl
from jax.experimental.pallas import tpu as pltpu
from jax.sharding import PartitionSpec as P

MESH = pl.DeviceIdType.MESH
HBM = pl.ANY
VMEM = pltpu.VMEM
BF = jnp.bfloat16
F32 = jnp.float32
BLK = 128
HEADS = 20
LOG2E = 1.4426950408889634
SCALE = 128 ** -0.5
FAR = 1e30
GROUP = 4 * BLK
VMEM_LIMIT = 60 * 2**20


def coords():
    c = lax.axis_index("ctx")
    return c // 8, (c // 2) % 4, c % 2, lax.axis_index("head")


def dev(x, z, k, y):
    return (x * 8 + z * 2 + k, y)


def rows(start, size):
    return pl.ds(pl.multiple_of(start, BLK), size)


def cols(head):
    return pl.ds(pl.multiple_of(head * BLK, BLK), BLK)


def q_pair(z):
    return z + 1 - 2 * (z % 2)


def k_pair(z):
    return (z + 3 + 2 * (z % 2)) % 4


def send(src, dst, ss, rs, to):
    pltpu.make_async_remote_copy(
        src_ref=src, dst_ref=dst, send_sem=ss, recv_sem=rs, device_id=to, device_id_type=MESH
    ).start()


def wait(ref, sem):
    pltpu.make_async_copy(ref, ref, sem).wait()


def greet():
    x, z, k, y = coords()
    barrier = pltpu.get_barrier_semaphore()
    peers = [dev((x + dx) % 4, z, k, (y + dy) % 4) for dx in range(4) for dy in range(4) if dx or dy]
    peers += [dev(x, (z + dz) % 4, k, y) for dz in range(1, 4)]
    peers.append(dev(x, z, 1 - k, y))
    for peer in peers:
        pl.semaphore_signal(barrier, inc=1, device_id=peer, device_id_type=MESH)
    pl.semaphore_wait(barrier, len(peers))


AHEAD = 6
ORDER = (1, 3, 2, 0)
BSTEP = 3
SPLIT = 4


def gather_kernel(
    q_in, k_in, v_in, g_in, o_in, norm_in, pat_in, order_in,
    qa, ga, xa, ka, va, qb, gb, xb, kb, vb, table,
    g_v, o_v, aux, pat_v, own_v, own_sem,
    load_sem, sa1, ra1, sb1, rb1, s_zq, r_zq, s_c, r_c, s_c2, r_c2, s_zk, r_zk,
    s_bz, r_bz, s_bc, r_bc, s_bx, r_bx,
):
    x, z, k, y = coords()
    load_g = pltpu.make_async_copy(g_in, g_v, load_sem.at[0])
    load_o = pltpu.make_async_copy(o_in, o_v, load_sem.at[1])
    load_g.start()
    load_o.start()
    own_loads = [
        pltpu.make_async_copy(ref.at[:, cols(head)], own_v.at[i * 4 + a], own_sem.at[i * 4 + a])
        for i, head in enumerate((y * 4 + x, 16 + y))
        for a, ref in enumerate((q_in, g_in, k_in, v_in))
    ]
    for load in own_loads:
        load.start()
    greet()
    mine = (x * 4 + y) * BLK

    slot = k * 4 + z
    wide = {0: (q_in, qa, qb), 1: (g_in, ga, gb), 2: (k_in, ka, kb), 3: (v_in, va, vb), 4: (aux, xa, xb)}

    def cut(a, head):
        src = wide[a][0]
        return src.at[head] if a == 4 else src.at[:, cols(head)]

    def scatter_a(a, wave):
        dst = xa.at[x * 4 + y] if a == 4 else wide[a][1].at[rows(mine, BLK), :]
        dx = wave
        for dy in (2, 1, 3, 0):
            tx, ty = (x + dx) % 4, (y + dy) % 4
            src = cut(a, ty * 4 + tx)
            if dx or dy:
                send(src, dst, sa1.at[a], ra1.at[a, wave], dev(tx, z, k, ty))
            else:
                if a < 4:
                    own_loads[a].wait()
                    src = own_v.at[a]
                pltpu.make_async_copy(src, dst, ra1.at[a, wave]).start()

    def scatter_b(a):
        if a == 4:
            dst = xb.at[slot * 4 + y]
        else:
            dst = wide[a][2].at[rows((slot if a < 2 else x) * GROUP + y * BLK, BLK), :]
        for dy in range(4):
            ty = (y + dy) % 4
            if dy:
                send(cut(a, 16 + ty), dst, sb1.at[a], rb1.at[a], dev(x, z, k, ty))
            else:
                if a < 4:
                    own_loads[4 + a].wait()
                src = own_v.at[4 + a] if a < 4 else cut(a, 16 + ty)
                pltpu.make_async_copy(src, dst, rb1.at[a]).start()

    steps = [(a, wave) for wave in (2, 1, 3, 0) for a in (0, 2, 1, 3)]
    for a in (0, 2, 1, 3):
        scatter_b(a)
    for step in steps[:AHEAD]:
        scatter_a(*step)

    load_g.wait()
    load_o.wait()
    for h in range(HEADS):
        prod = g_v[:, h * BLK:(h + 1) * BLK].astype(F32) * o_v[:, h * BLK:(h + 1) * BLK].astype(F32)
        dot = jnp.sum(prod.T, axis=0, keepdims=True)
        aux[h] = jnp.concatenate([norm_in[h:h + 1] * LOG2E, dot, jnp.zeros((6, BLK), F32)], axis=0)

    for wave in range(4):
        scatter_a(4, wave)
    scatter_b(4)

    def part(a, ref, quad, dx):
        at = quad * 4 + (x + 4 - dx) % 4
        return ref.at[pl.ds(at * 4, 4)] if a == 4 else ref.at[rows(at * GROUP, GROUP), :]

    def whole(a, ref, count=4):
        return ref.at[pl.ds(0, count)] if a == 4 else ref.at[pl.ds(0, count * BLK), :]

    buf_a = {0: qa, 1: ga, 2: ka, 3: va, 4: xa}
    buf_b = {0: qb, 1: gb, 2: kb, 3: vb, 4: xb}
    to_q = dev(x, q_pair(z), k, y)
    to_k = dev(x, k_pair(z), k, y)
    to_c = dev(x, z, 1 - k, y)

    def forward_a(a, dx):
        ref = buf_a[a]
        own, there = part(a, ref, 0, dx), part(a, ref, 1, dx)
        wait(own, ra1.at[a, dx])
        if a in (2, 3):
            send(own, there, s_zk.at[a - 2], r_zk.at[a - 2], to_k)
        else:
            send(own, there, s_zq.at[a], r_zq.at[a, dx], to_q)
            send(own, part(a, ref, 2, dx), s_c.at[a], r_c.at[a], to_c)

    def slab(a, ref, index, count=1):
        if a == 4:
            return ref.at[pl.ds(index * 4, 4 * count)]
        return ref.at[rows(index * GROUP, GROUP * count), :]

    def forward_b():
        for a in (0, 1, 4):
            ref = buf_b[a]
            own = slab(a, ref, slot)
            wait(own, rb1.at[a])
            for dz in (1, 3, 2):
                send(own, own, s_bz.at[a], r_bz.at[a, dz], dev(x, (z + dz) % 4, k, y))
            send(own, own, s_bc.at[a], r_bc.at[a], to_c)
        for a in (2, 3):
            ref = buf_b[a]
            own = slab(a, ref, x)
            wait(own, rb1.at[a])
            for dx in (1, 3, 2):
                send(own, own, s_bx.at[a - 2], r_bx.at[a - 2], dev((x + dx) % 4, z, k, y))

    for n, step in enumerate(steps):
        if n == BSTEP:
            forward_b()
        forward_a(*step)
        if n + AHEAD < 16:
            scatter_a(*steps[n + AHEAD])
    for wave in range(4):
        forward_a(4, wave)

    pat_v[...] = jnp.full((BLK, BLK), -1.0, F32)
    pat_v[0:36, :] = pat_in[...].astype(F32)
    order = jnp.broadcast_to(order_in[...].astype(F32), (BLK, BLK))
    i0 = lax.broadcasted_iota(jnp.int32, (BLK, BLK), 0)
    i1 = lax.broadcasted_iota(jnp.int32, (BLK, BLK), 1)
    hot = jnp.where(i0.astype(F32) == order, 1.0, 0.0)
    pat_v[...] = jnp.dot(pat_v[...].astype(BF), hot.astype(BF), preferred_element_type=F32)
    order_t = order.T
    adj = jnp.zeros((BLK, BLK), F32)
    for e in range(36):
        adj = jnp.where(pat_v[e:e + 1, :] == order_t, 1.0, adj)
    adj = adj.T
    local = (i0 // 4) == (i1 // 4)
    pick = jnp.where((i0 // 4) == i1, (i0 % 4 + 1).astype(F32), 0.0)
    own_cols = jnp.where(i1 == 32 + i0 % 4, 1.0, 0.0)
    table[...] = (
        jnp.dot(jnp.where(local, 0.0, adj).astype(BF), pick.astype(BF), preferred_element_type=F32)
        + jnp.dot(jnp.where(local, adj, 0.0).astype(BF), own_cols.astype(BF), preferred_element_type=F32)
    ).astype(jnp.int32)

    for dz in (1, 3, 2):
        for a in (0, 1, 4):
            ref = buf_b[a]
            got = slab(a, ref, k * 4 + (z + 4 - dz) % 4)
            wait(got, r_bz.at[a, dz])
            send(got, got, s_bc.at[a], r_bc.at[a], to_c)
    for wave in (2, 1, 3, 0):
        for a in (0, 1, 4):
            ref = buf_a[a]
            wait(part(a, ref, 1, wave), r_zq.at[a, wave])
            send(part(a, ref, 1, wave), part(a, ref, 3, wave), s_c2.at[a], r_c2.at[a], to_c)

    def quad(a, ref, index):
        if a == 4:
            return ref.at[pl.ds(index * 16, 16)]
        return ref.at[pl.ds(index * 4 * GROUP, 4 * GROUP), :]

    for a in (2, 3):
        wait(quad(a, buf_a[a], 1), r_zk.at[a - 2])
        wait(quad(a, buf_a[a], 0), s_zk.at[a - 2])
        wait(slab(a, buf_b[a], 0, 3), r_bx.at[a - 2])
        wait(slab(a, buf_b[a], 0, 3), s_bx.at[a - 2])
    for a in (0, 1, 4):
        wait(quad(a, buf_a[a], 2), r_c.at[a])
        wait(quad(a, buf_a[a], 3), r_c2.at[a])
        wait(quad(a, buf_a[a], 0), s_zq.at[a])
        wait(quad(a, buf_a[a], 0), s_c.at[a])
        wait(quad(a, buf_a[a], 0), s_c2.at[a])
        wait(slab(a, buf_b[a], 0, 4), r_bc.at[a])
        wait(slab(a, buf_b[a], 0, 4), s_bc.at[a])
        wait(slab(a, buf_b[a], 0, 3), s_bz.at[a])
    for a in range(5):
        ref = buf_a[a]
        if a == 4:
            wait(ref.at[pl.ds(0, 15)], sa1.at[a])
            wait(ref.at[pl.ds(0, 3)], sb1.at[a])
        else:
            wait(ref.at[pl.ds(0, 15 * BLK), :], sa1.at[a])
            wait(ref.at[pl.ds(0, 3 * BLK), :], sb1.at[a])


def compute_kernel(
    table, qa_in, ga_in, xa_in, ka_in, va_in, qb_in, gb_in, xb_in, kb_in, vb_in,
    dqa_out, dka_out, dva_out, dqb_out, dkb_out, dvb_out,
    qa, ga, xa, ka, va, qb, gb, xb, kb, vb, dqa, dka, dva, dqb, dkb, dvb, in_sem, out_sem,
    acc_k, acc_v, kt_ref, s_ref, d_ref, p_ref, e_ref,
):
    x, z, k, y = coords()
    base2 = SCALE * LOG2E
    zq, zk = q_pair(z), k_pair(z)
    pairs_in = [
        (ka_in, ka), (va_in, va), (qa_in, qa), (ga_in, ga), (xa_in, xa),
        (kb_in, kb), (vb_in, vb), (qb_in, qb), (gb_in, gb), (xb_in, xb),
    ]
    loads = [pltpu.make_async_copy(src, dst, in_sem.at[i]) for i, (src, dst) in enumerate(pairs_in)]
    for load in loads[:5]:
        load.start()
    stores = []

    def store(src, dst):
        copy = pltpu.make_async_copy(src, dst, out_sem.at[len(stores)])
        copy.start()
        stores.append(copy)

    def lanes(x_ref, q, row):
        return jnp.concatenate([x_ref[q * 4 + b, row:row + 1, :] for b in range(4)], axis=1)

    def blocks(ref, places, axis=0):
        return jnp.concatenate([ref[pl.ds(p, BLK), :] for p in places], axis=axis)

    def span(q):
        return pl.ds(pl.multiple_of(q * GROUP, GROUP), GROUP)

    def picked(c, groups):
        places, biases = [], []
        for first, key_index in groups:
            for i in range(4):
                code = table[4 * c, key_index(i)]
                places.append(pl.multiple_of((first + i) * GROUP + jnp.maximum(code - 1, 0) * BLK, BLK))
                biases.append(jnp.where(code > 0, 0.0, FAR))
        return places, biases

    def soften(score, dprob, norm, dot, hide=None):
        prob = jnp.exp2(score * base2 - norm)
        if hide is not None:
            prob = jnp.where(hide, 0.0, prob)
        return prob.astype(BF), (prob * (dprob - dot)).astype(BF)

    def stage_1(q_ref, g_ref, k_ref, v_ref, q, places, s, d):
        s[...] = jnp.dot(blocks(k_ref, places), q_ref[span(q), :].T, preferred_element_type=F32)
        d[...] = jnp.dot(blocks(v_ref, places), g_ref[span(q), :].T, preferred_element_type=F32)

    def stage_2(x_ref, q, biases, s, d, p, e):
        norm, dot = lanes(x_ref, q, 0), lanes(x_ref, q, 1)
        for i, bias in enumerate(biases):
            cut = slice(i * BLK, (i + 1) * BLK)
            p[cut, :], e[cut, :] = soften(s[cut, :], d[cut, :], norm + bias, dot)

    def stage_3(q_ref, g_ref, dq_ref, q, places, p, e):
        dk = jnp.dot(e[...], q_ref[span(q), :], preferred_element_type=F32)
        dv = jnp.dot(p[...], g_ref[span(q), :], preferred_element_type=F32)
        dq = jnp.dot(blocks(kt_ref, places, 1), e[...], preferred_element_type=F32)
        for i, at in enumerate(places):
            inner = pl.ds(pl.multiple_of(at - i * GROUP, BLK), BLK)
            acc_k[i][inner, :] += dk[i * BLK:(i + 1) * BLK]
            acc_v[i][inner, :] += dv[i * BLK:(i + 1) * BLK]
        dq_ref[span(q), :] = (dq * SCALE).T.astype(BF)

    def turn(k_ref, n):
        def step(i, carry):
            turned = k_ref[span(i), :].T
            for b in range(4):
                kt_ref[rows(i * GROUP + b * BLK, BLK), :] = turned[:, b * BLK:(b + 1) * BLK]
            return carry

        lax.fori_loop(0, n // 4, step, 0)

    def finish(dk_ref, dv_ref, n):
        for i in range(n):
            at = pl.ds(i * GROUP, GROUP)
            dk_ref[at, :] = (acc_k[i][...] * SCALE).astype(BF)
            dv_ref[at, :] = acc_v[i][...].astype(BF)

    def main(q_ref, g_ref, x_ref, k_ref, v_ref, dq_ref, count, c_of, groups):
        n = len(groups) * GROUP
        s, d = s_ref.at[:, 0:n, :], d_ref.at[:, 0:n, :]
        p, e = p_ref.at[:, 0:n, :], e_ref.at[:, 0:n, :]

        def one(t, half, stages):
            now, then = half, 1 - half
            if 3 in stages:
                places3, _ = picked(c_of(t - 2), groups)
                stage_3(q_ref, g_ref, dq_ref, t - 2, places3, p.at[now], e.at[now])
            if 1 in stages:
                places1, _ = picked(c_of(t), groups)
                stage_1(q_ref, g_ref, k_ref, v_ref, t, places1, s.at[now], d.at[now])
            if 2 in stages:
                _, biases2 = picked(c_of(t - 1), groups)
                stage_2(x_ref, t - 1, biases2, s.at[then], d.at[then], p.at[then], e.at[then])

        def step(it, carry):
            for half in range(2):
                one(2 * it + half, half, (1, 2, 3))
            return carry

        one(0, 0, (1,))
        one(1, 1, (1, 2))
        lax.fori_loop(1, count // 2, step, 0)
        one(count, 0, (2, 3))
        one(count + 1, 1, (3,))

    def diag(q_ref, g_ref, x_ref, k_ref, v_ref, dq_ref, q, c, own):
        here = span(own)
        places = [pl.multiple_of(own * GROUP + b * BLK, BLK) for b in range(4)]
        query, grad = q_ref[span(q), :], g_ref[span(q), :]
        score = jnp.dot(k_ref[here, :], query.T, preferred_element_type=F32)
        dprob = jnp.dot(v_ref[here, :], grad.T, preferred_element_type=F32)
        norm, dot = lanes(x_ref, q, 0), lanes(x_ref, q, 1)
        probs, scores = [], []
        key_at = lax.broadcasted_iota(jnp.int32, (BLK, GROUP), 0)
        query_at = lax.broadcasted_iota(jnp.int32, (BLK, GROUP), 1)
        for i in range(4):
            bias = jnp.concatenate(
                [
                    jnp.full((1, BLK), jnp.where(table[4 * c + b, 32 + i] > 0, 0.0, FAR), F32)
                    for b in range(4)
                ],
                axis=1,
            )
            hide = (query_at >= i * BLK) & (query_at < key_at + i * BLK)
            cut = slice(i * BLK, (i + 1) * BLK)
            prob, score_e = soften(score[cut], dprob[cut], norm + bias, dot, hide)
            probs.append(prob)
            scores.append(score_e)
        prob = jnp.concatenate(probs, axis=0)
        score = jnp.concatenate(scores, axis=0)
        dk = jnp.dot(score, query, preferred_element_type=F32)
        dv = jnp.dot(prob, grad, preferred_element_type=F32)
        if isinstance(own, int):
            acc_k[own][...] += dk
            acc_v[own][...] += dv
        else:
            for i in range(4):
                @pl.when(own == i)
                def _(i=i):
                    acc_k[i][...] += dk
                    acc_v[i][...] += dv
        dq = jnp.dot(blocks(kt_ref, places, 1), score, preferred_element_type=F32)
        dq_ref[span(q), :] = (dq_ref[span(q), :].astype(F32) + (dq * SCALE).T).astype(BF)

    def clear(n):
        for ref in (*acc_k[:n], *acc_v[:n]):
            ref[...] = jnp.zeros((GROUP, BLK), F32)

    clear(8)

    def index_a(q):
        quad, xq = q // 4, q % 4
        zc = jnp.where(quad % 2 == 0, z, zq)
        kc = jnp.where(quad < 2, k, 1 - k)
        return xq * 8 + zc * 2 + kc

    loads[0].wait()
    turn(ka, 32)
    for load in loads[1:5]:
        load.wait()
    for load in loads[5:]:
        load.start()
    main(qa, ga, xa, ka, va, dqa, 16, index_a, [(0, lambda i: i * 8 + z * 2 + k), (4, lambda i: i * 8 + zk * 2 + k)])

    late = pl.ds(4 * GROUP, 12 * GROUP)
    store(dqa.at[late, :], dqa_out.at[late, :])

    for q in range(4):
        diag(qa, ga, xa, ka, va, dqa, q, index_a(q), q)
    early = pl.ds(0, 4 * GROUP)
    store(dqa.at[early, :], dqa_out.at[early, :])
    finish(dka, dva, 8)
    store(dka, dka_out)
    store(dva, dva_out)
    for load in loads[5:]:
        load.wait()

    clear(4)
    turn(kb, 16)
    main(qb, gb, xb, kb, vb, dqb, 8, lambda q: x * 8 + (q % 4) * 2 + q // 4, [(0, lambda i: i * 8 + z * 2 + k)])
    diag(qb, gb, xb, kb, vb, dqb, k * 4 + z, x * 8 + z * 2 + k, x)
    store(dqb, dqb_out)
    finish(dkb, dvb, 4)
    store(dkb, dkb_out)
    store(dvb, dvb_out)
    for copy in stores:
        copy.wait()


def compute_call(table, *gathered):
    wide = lambda n: jax.ShapeDtypeStruct((n * BLK, BLK), BF)
    any_ = pl.BlockSpec(memory_space=HBM)
    hold = lambda n: VMEM((n * BLK, BLK), BF)
    aux = lambda n: VMEM((n, 8, BLK), F32)
    return pl.pallas_call(
        compute_kernel,
        out_shape=(wide(64), wide(32), wide(32), wide(32), wide(16), wide(16)),
        in_specs=[pl.BlockSpec(memory_space=pltpu.SMEM)] + [any_] * 10,
        out_specs=(any_,) * 6,
        scratch_shapes=[
            hold(64), hold(64), aux(64), hold(32), hold(32), hold(32), hold(32), aux(32), hold(16), hold(16),
            hold(64), hold(32), hold(32), hold(32), hold(16), hold(16),
            pltpu.SemaphoreType.DMA((10,)), pltpu.SemaphoreType.DMA((7,)),
            [VMEM((GROUP, BLK), F32)] * 8, [VMEM((GROUP, BLK), F32)] * 8, hold(32),
            VMEM((2, 8 * BLK, GROUP), F32), VMEM((2, 8 * BLK, GROUP), F32),
            VMEM((2, 8 * BLK, GROUP), BF), VMEM((2, 8 * BLK, GROUP), BF),
        ],
        compiler_params=pltpu.CompilerParams(vmem_limit_bytes=VMEM_LIMIT),
        name="block_grads",
    )(table, *gathered)


def return_kernel(
    dqa, dka, dva, dqb, dkb, dvb,
    dq_out, dk_out, dv_out,
    own_q, own_k, own_v, own_bq, own_bk, own_bv, own_sem,
    got_zk, got_c, got_zq, put_zq, fin, bgot_c, bput_q, bgot_z, bgot_x, bfin,
    s_zk, r_zk, s_c, r_c, s_zq, r_zq, s_bc, r_bc, s_bz, r_bz, s_bx, r_bx, s_out, r_out,
):
    x, z, k, y = coords()
    outs = (dq_out, dk_out, dv_out)
    to_q = dev(x, q_pair(z), k, y)
    to_k = dev(x, k_pair(z), k, y)
    to_c = dev(x, z, 1 - k, y)
    half, quarter = pl.ds(0, 4 * GROUP), rows(x * GROUP, GROUP)
    loads = [
        pltpu.make_async_copy(src, dst, own_sem.at[i])
        for i, (src, dst) in enumerate([
            (dqa.at[pl.ds(0, 8 * GROUP), :], own_q),
            (dqb.at[rows(k * 4 * GROUP, 4 * GROUP), :], own_bq),
            (dka.at[half, :], own_k), (dva.at[half, :], own_v),
            (dkb.at[quarter, :], own_bk), (dvb.at[quarter, :], own_bv),
        ])
    ]
    for load in loads:
        load.start()
    greet()

    def chunk(ref, quad, dx):
        return ref.at[rows((quad * 4 + (x + dx) % 4) * GROUP, GROUP), :]

    def slab(ref, index):
        return ref.at[rows(index * GROUP, GROUP), :]

    def add(*refs):
        total = refs[0][...].astype(F32)
        for ref in refs[1:]:
            total = total + ref[...].astype(F32)
        return total.astype(BF)

    def give(n, src, base, tx, head_of, dx):
        for dy in range(4):
            ty = (y + dy) % 4
            block = src.at[rows(base + ty * BLK, BLK), :]
            dst = outs[n].at[:, cols(head_of)]
            if dx or dy:
                send(block, dst, s_out.at[n], r_out.at[n], dev(tx, z, k, ty))
            else:
                pltpu.make_async_copy(block, dst, r_out.at[n]).start()

    def keys_out(dx):
        for n, src in enumerate((dka, dva)):
            send(chunk(src, 1, dx), chunk(got_zk.at[n], 0, dx), s_zk, r_zk.at[n, dx], to_k)

    def far_keys_out(dx):
        for n, src in enumerate((dkb, dvb)):
            to = dev((x + dx) % 4, z, k, y)
            send(slab(src, (x + dx) % 4), slab(bgot_x.at[n], dx - 1), s_bx, r_bx.at[n, dx - 1], to)

    def queries_on(dx):
        wait(chunk(got_c, 1, dx), r_c.at[1, dx])
        part = chunk(put_zq, 0, dx)
        part[...] = add(chunk(own_q, 1, dx), chunk(got_c, 1, dx))
        send(part, chunk(got_zq, 0, dx), s_zq, r_zq.at[dx], to_q)

    def far_queries_on(dz):
        zt = (z + dz) % 4
        part = slab(bput_q, zt)
        part[...] = add(slab(own_bq, zt), slab(bgot_c, zt))
        send(part, slab(bgot_z, dz - 1), s_bz, r_bz.at[dz - 1], dev(x, zt, k, y))

    def keys_home(dx):
        tx = (x + dx) % 4
        for n, own in ((1, own_k), (2, own_v)):
            wait(chunk(got_zk.at[n - 1], 0, dx), r_zk.at[n - 1, dx])
            out = chunk(fin.at[n], 0, dx)
            out[...] = add(chunk(own, 0, dx), chunk(got_zk.at[n - 1], 0, dx))
            give(n, fin.at[n], tx * GROUP, tx, y * 4 + x, dx)

    def queries_home(dx):
        tx = (x + dx) % 4
        wait(chunk(got_c, 0, dx), r_c.at[0, dx])
        wait(chunk(got_zq, 0, dx), r_zq.at[dx])
        out = chunk(fin.at[0], 0, dx)
        out[...] = add(chunk(own_q, 0, dx), chunk(got_c, 0, dx), chunk(got_zq, 0, dx))
        give(0, fin.at[0], tx * GROUP, tx, y * 4 + x, dx)

    def far_keys_home():
        for n, own in ((1, own_bk), (2, own_bv)):
            for i in range(3):
                wait(slab(bgot_x.at[n - 1], i), r_bx.at[n - 1, i])
            bfin[n] = add(own, *[slab(bgot_x.at[n - 1], i) for i in range(3)])
            give(n, bfin.at[n], 0, x, 16 + y, 0)

    def far_queries_home():
        for i in range(3):
            wait(slab(bgot_z, i), r_bz.at[i])
        bfin[0] = add(slab(own_bq, z), slab(bgot_c, z), *[slab(bgot_z, i) for i in range(3)])
        give(0, bfin.at[0], 0, x, 16 + y, 0)

    first, second, third, last = ORDER
    for dx in ORDER:
        send(chunk(dqa, 3, dx), chunk(got_c, 1, dx), s_c, r_c.at[1, dx], to_c)
    send(dqb.at[rows((1 - k) * 4 * GROUP, 4 * GROUP), :], bgot_c, s_bc, r_bc, to_c)
    keys_out(first)
    far_keys_out(1)
    far_keys_out(3)
    for load in loads:
        load.wait()
    for dx in ORDER:
        send(chunk(dqa, 2, dx), chunk(got_c, 0, dx), s_c, r_c.at[0, dx], to_c)
    for dx in ORDER:
        queries_on(dx)
    far_keys_out(2)
    for dx in ORDER[1:]:
        keys_out(dx)
    wait(bgot_c, r_bc)
    for dz in (1, 3, 2):
        far_queries_on(dz)
    for dx in ORDER:
        queries_home(dx)
        keys_home(dx)
        if dx == 1:
            far_keys_home()
    far_queries_home()

    for n in range(3):
        wait(outs[n], r_out.at[n])
        wait(dqa.at[pl.ds(0, 18 * BLK), :], s_out.at[n])
    wait(dqa.at[pl.ds(0, 8 * GROUP), :], s_c)
    wait(dqa.at[pl.ds(0, 8 * GROUP), :], s_zk)
    wait(put_zq, s_zq)
    wait(bgot_c, s_bc)
    wait(bgot_z, s_bz)
    wait(dqa.at[pl.ds(0, 6 * GROUP), :], s_bx)


def hand_out_kernel(dq, dk, dv, dq_out, dk_out, dv_out, held, sems):
    part = dq.shape[0] // SPLIT
    pieces = [(n, i) for i in range(SPLIT) for n in range(3)]
    src, dst = (dq, dk, dv), (dq_out, dk_out, dv_out)

    def cut(ref, i):
        return ref.at[pl.ds(i * part, part), :]

    loads = [pltpu.make_async_copy(cut(src[n], i), cut(held.at[n], i), sems.at[0, n, i]) for n, i in pieces]
    stores = [pltpu.make_async_copy(cut(held.at[n], i), cut(dst[n], i), sems.at[1, n, i]) for n, i in pieces]
    for load in loads:
        load.start()
    for load, store in zip(loads, stores):
        load.wait()
        store.start()
    for store in stores:
        store.wait()


def body(queries, key_rows, value_rows, forward_out, out_grad, log_norm, block_order, pattern):
    wide = lambda n: jax.ShapeDtypeStruct((n * BLK, BLK), BF)
    aux = lambda n: jax.ShapeDtypeStruct((n, 8, BLK), F32)
    any_ = pl.BlockSpec(memory_space=HBM)
    vmem = pl.BlockSpec(memory_space=VMEM)
    sem = lambda *shape: pltpu.SemaphoreType.DMA(shape)
    one = pltpu.SemaphoreType.DMA
    hold = lambda n: VMEM((n * BLK, BLK), BF)
    tokens, width = queries.shape

    gathered = pl.pallas_call(
        gather_kernel,
        out_shape=(
            wide(64), wide(64), aux(64), wide(32), wide(32),
            wide(32), wide(32), aux(32), wide(16), wide(16),
            jax.ShapeDtypeStruct((BLK, BLK), jnp.int32),
        ),
        in_specs=[any_] * 5 + [vmem] * 3,
        out_specs=(any_,) * 10 + (vmem,),
        scratch_shapes=[
            VMEM((tokens, width), BF), VMEM((tokens, width), BF), VMEM((HEADS, 8, BLK), F32),
            VMEM((BLK, BLK), F32), VMEM((8, BLK, BLK), BF), sem(8),
            sem(2), sem(5), sem(5, 4), sem(5), sem(5), sem(5), sem(5, 4), sem(5), sem(5), sem(5), sem(5), sem(2), sem(2),
            sem(5), sem(5, 4), sem(5), sem(5), sem(2), sem(2),
        ],
        compiler_params=pltpu.CompilerParams(
            collective_id=0, has_side_effects=True, vmem_limit_bytes=VMEM_LIMIT
        ),
        name="gather_blocks",
    )(
        queries, key_rows, value_rows, out_grad, forward_out, log_norm.T, pattern.T,
        block_order.reshape(1, BLK),
    )
    table = gathered[-1]

    grads = compute_call(table, *gathered[:10])
    flat = jax.ShapeDtypeStruct((tokens, width), BF)
    landed = pl.pallas_call(
        return_kernel,
        out_shape=(flat, flat, flat),
        in_specs=[any_] * 6,
        out_specs=(any_,) * 3,
        scratch_shapes=[
            hold(32), hold(16), hold(16), hold(16), hold(4), hold(4), sem(6),
            VMEM((2, 16 * BLK, BLK), BF), VMEM((32 * BLK, BLK), BF), VMEM((16 * BLK, BLK), BF),
            VMEM((16 * BLK, BLK), BF), VMEM((3, 16 * BLK, BLK), BF),
            VMEM((16 * BLK, BLK), BF), VMEM((16 * BLK, BLK), BF), VMEM((12 * BLK, BLK), BF),
            VMEM((2, 12 * BLK, BLK), BF), VMEM((3, GROUP, BLK), BF),
            one, sem(2, 4), one, sem(2, 4), one, sem(4), one, one, one, sem(3), one, sem(2, 3), sem(3), sem(3),
        ],
        compiler_params=pltpu.CompilerParams(
            collective_id=1, has_side_effects=True, vmem_limit_bytes=VMEM_LIMIT
        ),
        name="return_grads",
    )(*grads)
    return pl.pallas_call(
        hand_out_kernel,
        out_shape=(flat, flat, flat),
        in_specs=[any_] * 3,
        out_specs=(any_,) * 3,
        scratch_shapes=[VMEM((3, tokens, width), BF), sem(2, 3, SPLIT)],
        compiler_params=pltpu.CompilerParams(vmem_limit_bytes=VMEM_LIMIT),
        name="hand_out",
    )(*landed)


def solution(mesh):
    tokens = P(("ctx", "head"), None)
    return jax.shard_map(
        body,
        mesh=mesh,
        in_specs=(tokens,) * 6 + (P(), P()),
        out_specs=(tokens,) * 3,
        check_vma=False,
    )
```

```python
import functools

import jax
import jax.numpy as jnp
from jax import lax
from jax.experimental import pallas as pl
from jax.experimental.pallas import tpu as pltpu
from jax.sharding import PartitionSpec as P

MESH = pl.DeviceIdType.MESH
HBM = pl.ANY
VMEM = pltpu.VMEM
BF = jnp.bfloat16
F32 = jnp.float32
BLK = 128
HEADS = 20
LOG2E = 1.4426950408889634
SCALE = 128 ** -0.5
FAR = 1e30
GROUP = 4 * BLK
VMEM_LIMIT = 60 * 2**20


def coords():
    c = lax.axis_index("ctx")
    return c // 8, (c // 2) % 4, c % 2, lax.axis_index("head")


def dev(x, z, k, y):
    return (x * 8 + z * 2 + k, y)


def rows(start, size):
    return pl.ds(pl.multiple_of(start, BLK), size)


def cols(head):
    return pl.ds(pl.multiple_of(head * BLK, BLK), BLK)


def q_pair(z):
    return z + 1 - 2 * (z % 2)


def k_pair(z):
    return (z + 3 + 2 * (z % 2)) % 4


def send(src, dst, ss, rs, to):
    pltpu.make_async_remote_copy(
        src_ref=src, dst_ref=dst, send_sem=ss, recv_sem=rs, device_id=to, device_id_type=MESH
    ).start()


def wait(ref, sem):
    pltpu.make_async_copy(ref, ref, sem).wait()


def greet():
    x, z, k, y = coords()
    barrier = pltpu.get_barrier_semaphore()
    peers = [dev((x + dx) % 4, z, k, (y + dy) % 4) for dx in range(4) for dy in range(4) if dx or dy]
    peers += [dev(x, (z + dz) % 4, k, y) for dz in range(1, 4)]
    peers.append(dev(x, z, 1 - k, y))
    for peer in peers:
        pl.semaphore_signal(barrier, inc=1, device_id=peer, device_id_type=MESH)
    pl.semaphore_wait(barrier, len(peers))


AHEAD = 6
ORDER = (1, 3, 2, 0)
BSTEP = 3
RELAY = 11
SPLIT = 4


def gather_kernel(
    q_in, k_in, v_in, g_in, o_in, norm_in, pat_in, order_in,
    qa, ga, xa, ka, va, qb, gb, xb, kb, vb, table,
    g_v, o_v, aux, pat_v, own_v, own_sem,
    load_sem, sa1, ra1, sb1, rb1, s_zq, r_zq, s_c, r_c, s_c2, r_c2, s_zk, r_zk,
    s_bz, r_bz, s_bc, r_bc, s_bx, r_bx,
):
    x, z, k, y = coords()
    load_g = pltpu.make_async_copy(g_in, g_v, load_sem.at[0])
    load_o = pltpu.make_async_copy(o_in, o_v, load_sem.at[1])
    load_g.start()
    load_o.start()
    own_loads = [
        pltpu.make_async_copy(ref.at[:, cols(head)], own_v.at[i * 4 + a], own_sem.at[i * 4 + a])
        for i, head in enumerate((y * 4 + x, 16 + y))
        for a, ref in enumerate((q_in, g_in, k_in, v_in))
    ]
    for load in own_loads:
        load.start()
    greet()
    mine = (x * 4 + y) * BLK

    slot = k * 4 + z
    wide = {0: (q_in, qa, qb), 1: (g_in, ga, gb), 2: (k_in, ka, kb), 3: (v_in, va, vb), 4: (aux, xa, xb)}

    def cut(a, head):
        src = wide[a][0]
        return src.at[head] if a == 4 else src.at[:, cols(head)]

    def scatter_a(a, wave):
        dst = xa.at[x * 4 + y] if a == 4 else wide[a][1].at[rows(mine, BLK), :]
        dx = wave
        for dy in (2, 1, 3, 0):
            tx, ty = (x + dx) % 4, (y + dy) % 4
            src = cut(a, ty * 4 + tx)
            if dx or dy:
                send(src, dst, sa1.at[a], ra1.at[a, wave], dev(tx, z, k, ty))
            else:
                if a < 4:
                    own_loads[a].wait()
                    src = own_v.at[a]
                pltpu.make_async_copy(src, dst, ra1.at[a, wave]).start()

    def scatter_b(a):
        if a == 4:
            dst = xb.at[slot * 4 + y]
        else:
            dst = wide[a][2].at[rows((slot if a < 2 else x) * GROUP + y * BLK, BLK), :]
        for dy in range(4):
            ty = (y + dy) % 4
            if dy:
                send(cut(a, 16 + ty), dst, sb1.at[a], rb1.at[a], dev(x, z, k, ty))
            else:
                if a < 4:
                    own_loads[4 + a].wait()
                src = own_v.at[4 + a] if a < 4 else cut(a, 16 + ty)
                pltpu.make_async_copy(src, dst, rb1.at[a]).start()

    steps = [(a, wave) for wave in (2, 1, 3, 0) for a in (0, 2, 1, 3)]
    for a in (0, 2, 1, 3):
        scatter_b(a)
    for step in steps[:AHEAD]:
        scatter_a(*step)

    load_g.wait()
    load_o.wait()
    for h in range(HEADS):
        prod = g_v[:, h * BLK:(h + 1) * BLK].astype(F32) * o_v[:, h * BLK:(h + 1) * BLK].astype(F32)
        dot = jnp.sum(prod.T, axis=0, keepdims=True)
        aux[h] = jnp.concatenate([norm_in[h:h + 1] * LOG2E, dot, jnp.zeros((6, BLK), F32)], axis=0)

    for wave in range(4):
        scatter_a(4, wave)
    scatter_b(4)

    def part(a, ref, quad, dx):
        at = quad * 4 + (x + 4 - dx) % 4
        return ref.at[pl.ds(at * 4, 4)] if a == 4 else ref.at[rows(at * GROUP, GROUP), :]

    def whole(a, ref, count=4):
        return ref.at[pl.ds(0, count)] if a == 4 else ref.at[pl.ds(0, count * BLK), :]

    buf_a = {0: qa, 1: ga, 2: ka, 3: va, 4: xa}
    buf_b = {0: qb, 1: gb, 2: kb, 3: vb, 4: xb}
    to_q = dev(x, q_pair(z), k, y)
    to_k = dev(x, k_pair(z), k, y)
    to_c = dev(x, z, 1 - k, y)

    def forward_a(a, dx):
        ref = buf_a[a]
        own, there = part(a, ref, 0, dx), part(a, ref, 1, dx)
        wait(own, ra1.at[a, dx])
        if a in (2, 3):
            send(own, there, s_zk.at[a - 2], r_zk.at[a - 2], to_k)
        else:
            send(own, there, s_zq.at[a], r_zq.at[a, dx], to_q)
            send(own, part(a, ref, 2, dx), s_c.at[a], r_c.at[a], to_c)

    def slab(a, ref, index, count=1):
        if a == 4:
            return ref.at[pl.ds(index * 4, 4 * count)]
        return ref.at[rows(index * GROUP, GROUP * count), :]

    def forward_b():
        for a in (0, 1, 4):
            ref = buf_b[a]
            own = slab(a, ref, slot)
            wait(own, rb1.at[a])
            for dz in (1, 3):
                send(own, own, s_bz.at[a], r_bz.at[a, dz], dev(x, (z + dz) % 4, k, y))
            send(own, own, s_bc.at[a], r_bc.at[a], to_c)
        for a in (2, 3):
            ref = buf_b[a]
            own = slab(a, ref, x)
            wait(own, rb1.at[a])
            for dx in (1, 3):
                send(own, own, s_bx.at[a - 2], r_bx.at[a - 2, dx], dev((x + dx) % 4, z, k, y))

    def half(a, ref, index, h):
        if a == 4:
            return ref.at[pl.ds(index * 4 + h * 2, 2)]
        return ref.at[rows(index * GROUP + h * 2 * BLK, 2 * BLK), :]

    def relay_b():
        for a in (0, 2, 1, 3, 4):
            ref = buf_b[a]
            for h, d in ((0, 1), (1, 3)):
                if a in (2, 3):
                    index = (x + 4 - d) % 4
                    wait(slab(a, ref, index), r_bx.at[a - 2, d])
                    piece = half(a, ref, index, h)
                    send(piece, piece, s_bx.at[a - 2], r_bx.at[a - 2, 2], dev((x + d) % 4, z, k, y))
                else:
                    index = k * 4 + (z + 4 - d) % 4
                    got = slab(a, ref, index)
                    wait(got, r_bz.at[a, d])
                    piece = half(a, ref, index, h)
                    send(piece, piece, s_bz.at[a], r_bz.at[a, 2], dev(x, (z + d) % 4, k, y))
                    send(got, got, s_bc.at[a], r_bc.at[a], to_c)

    for n, step in enumerate(steps):
        if n == BSTEP:
            forward_b()
        if n == RELAY:
            relay_b()
        forward_a(*step)
        if n + AHEAD < 16:
            scatter_a(*steps[n + AHEAD])
    for wave in range(4):
        forward_a(4, wave)

    pat_v[...] = jnp.full((BLK, BLK), -1.0, F32)
    pat_v[0:36, :] = pat_in[...].astype(F32)
    order = jnp.broadcast_to(order_in[...].astype(F32), (BLK, BLK))
    i0 = lax.broadcasted_iota(jnp.int32, (BLK, BLK), 0)
    i1 = lax.broadcasted_iota(jnp.int32, (BLK, BLK), 1)
    hot = jnp.where(i0.astype(F32) == order, 1.0, 0.0)
    pat_v[...] = jnp.dot(pat_v[...].astype(BF), hot.astype(BF), preferred_element_type=F32)
    order_t = order.T
    adj = jnp.zeros((BLK, BLK), F32)
    for e in range(36):
        adj = jnp.where(pat_v[e:e + 1, :] == order_t, 1.0, adj)
    adj = adj.T
    local = (i0 // 4) == (i1 // 4)
    pick = jnp.where((i0 // 4) == i1, (i0 % 4 + 1).astype(F32), 0.0)
    own_cols = jnp.where(i1 == 32 + i0 % 4, 1.0, 0.0)
    table[...] = (
        jnp.dot(jnp.where(local, 0.0, adj).astype(BF), pick.astype(BF), preferred_element_type=F32)
        + jnp.dot(jnp.where(local, adj, 0.0).astype(BF), own_cols.astype(BF), preferred_element_type=F32)
    ).astype(jnp.int32)

    for a in (0, 1, 4):
        ref = buf_b[a]
        got = slab(a, ref, k * 4 + (z + 2) % 4)
        wait(got, r_bz.at[a, 2])
        send(got, got, s_bc.at[a], r_bc.at[a], to_c)
    for wave in (2, 1, 3, 0):
        for a in (0, 1, 4):
            ref = buf_a[a]
            wait(part(a, ref, 1, wave), r_zq.at[a, wave])
            send(part(a, ref, 1, wave), part(a, ref, 3, wave), s_c2.at[a], r_c2.at[a], to_c)

    def quad(a, ref, index):
        if a == 4:
            return ref.at[pl.ds(index * 16, 16)]
        return ref.at[pl.ds(index * 4 * GROUP, 4 * GROUP), :]

    for a in (2, 3):
        wait(quad(a, buf_a[a], 1), r_zk.at[a - 2])
        wait(quad(a, buf_a[a], 0), s_zk.at[a - 2])
        wait(slab(a, buf_b[a], 0), r_bx.at[a - 2, 2])
        wait(slab(a, buf_b[a], 0, 3), s_bx.at[a - 2])
    for a in (0, 1, 4):
        wait(quad(a, buf_a[a], 2), r_c.at[a])
        wait(quad(a, buf_a[a], 3), r_c2.at[a])
        wait(quad(a, buf_a[a], 0), s_zq.at[a])
        wait(quad(a, buf_a[a], 0), s_c.at[a])
        wait(quad(a, buf_a[a], 0), s_c2.at[a])
        wait(slab(a, buf_b[a], 0, 4), r_bc.at[a])
        wait(slab(a, buf_b[a], 0, 4), s_bc.at[a])
        wait(slab(a, buf_b[a], 0, 3), s_bz.at[a])
    for a in range(5):
        ref = buf_a[a]
        if a == 4:
            wait(ref.at[pl.ds(0, 15)], sa1.at[a])
            wait(ref.at[pl.ds(0, 3)], sb1.at[a])
        else:
            wait(ref.at[pl.ds(0, 15 * BLK), :], sa1.at[a])
            wait(ref.at[pl.ds(0, 3 * BLK), :], sb1.at[a])


def compute_kernel(
    table, qa_in, ga_in, xa_in, ka_in, va_in, qb_in, gb_in, xb_in, kb_in, vb_in,
    dqa_out, dka_out, dva_out, dqb_out, dkb_out, dvb_out,
    qa, ga, xa, ka, va, qb, gb, xb, kb, vb, dqa, dka, dva, dqb, dkb, dvb, in_sem, out_sem,
    acc_k, acc_v, kt_ref, s_ref, d_ref, p_ref, e_ref,
):
    x, z, k, y = coords()
    base2 = SCALE * LOG2E
    zq, zk = q_pair(z), k_pair(z)
    pairs_in = [
        (ka_in, ka), (va_in, va), (qa_in, qa), (ga_in, ga), (xa_in, xa),
        (kb_in, kb), (vb_in, vb), (qb_in, qb), (gb_in, gb), (xb_in, xb),
    ]
    loads = [pltpu.make_async_copy(src, dst, in_sem.at[i]) for i, (src, dst) in enumerate(pairs_in)]
    for load in loads[:5]:
        load.start()
    stores = []

    def store(src, dst):
        copy = pltpu.make_async_copy(src, dst, out_sem.at[len(stores)])
        copy.start()
        stores.append(copy)

    def lanes(x_ref, q, row):
        return jnp.concatenate([x_ref[q * 4 + b, row:row + 1, :] for b in range(4)], axis=1)

    def blocks(ref, places, axis=0):
        return jnp.concatenate([ref[pl.ds(p, BLK), :] for p in places], axis=axis)

    def span(q):
        return pl.ds(pl.multiple_of(q * GROUP, GROUP), GROUP)

    def picked(c, groups):
        places, biases = [], []
        for first, key_index in groups:
            for i in range(4):
                code = table[4 * c, key_index(i)]
                places.append(pl.multiple_of((first + i) * GROUP + jnp.maximum(code - 1, 0) * BLK, BLK))
                biases.append(jnp.where(code > 0, 0.0, FAR))
        return places, biases

    def soften(score, dprob, norm, dot, hide=None):
        prob = jnp.exp2(score * base2 - norm)
        if hide is not None:
            prob = jnp.where(hide, 0.0, prob)
        return prob.astype(BF), (prob * (dprob - dot)).astype(BF)

    def stage_1(q_ref, g_ref, k_ref, v_ref, q, places, s, d):
        s[...] = jnp.dot(blocks(k_ref, places), q_ref[span(q), :].T, preferred_element_type=F32)
        d[...] = jnp.dot(blocks(v_ref, places), g_ref[span(q), :].T, preferred_element_type=F32)

    def stage_2(x_ref, q, biases, s, d, p, e):
        norm, dot = lanes(x_ref, q, 0), lanes(x_ref, q, 1)
        for i, bias in enumerate(biases):
            cut = slice(i * BLK, (i + 1) * BLK)
            p[cut, :], e[cut, :] = soften(s[cut, :], d[cut, :], norm + bias, dot)

    def stage_3(q_ref, g_ref, dq_ref, q, places, p, e):
        dk = jnp.dot(e[...], q_ref[span(q), :], preferred_element_type=F32)
        dv = jnp.dot(p[...], g_ref[span(q), :], preferred_element_type=F32)
        dq = jnp.dot(blocks(kt_ref, places, 1), e[...], preferred_element_type=F32)
        for i, at in enumerate(places):
            inner = pl.ds(pl.multiple_of(at - i * GROUP, BLK), BLK)
            acc_k[i][inner, :] += dk[i * BLK:(i + 1) * BLK]
            acc_v[i][inner, :] += dv[i * BLK:(i + 1) * BLK]
        dq_ref[span(q), :] = (dq * SCALE).T.astype(BF)

    def turn(k_ref, n):
        def step(i, carry):
            turned = k_ref[span(i), :].T
            for b in range(4):
                kt_ref[rows(i * GROUP + b * BLK, BLK), :] = turned[:, b * BLK:(b + 1) * BLK]
            return carry

        lax.fori_loop(0, n // 4, step, 0)

    def finish(dk_ref, dv_ref, n):
        for i in range(n):
            at = pl.ds(i * GROUP, GROUP)
            dk_ref[at, :] = (acc_k[i][...] * SCALE).astype(BF)
            dv_ref[at, :] = acc_v[i][...].astype(BF)

    def main(q_ref, g_ref, x_ref, k_ref, v_ref, dq_ref, count, c_of, groups):
        n = len(groups) * GROUP
        s, d = s_ref.at[:, 0:n, :], d_ref.at[:, 0:n, :]
        p, e = p_ref.at[:, 0:n, :], e_ref.at[:, 0:n, :]

        def one(t, half, stages):
            now, then = half, 1 - half
            if 3 in stages:
                places3, _ = picked(c_of(t - 2), groups)
                stage_3(q_ref, g_ref, dq_ref, t - 2, places3, p.at[now], e.at[now])
            if 1 in stages:
                places1, _ = picked(c_of(t), groups)
                stage_1(q_ref, g_ref, k_ref, v_ref, t, places1, s.at[now], d.at[now])
            if 2 in stages:
                _, biases2 = picked(c_of(t - 1), groups)
                stage_2(x_ref, t - 1, biases2, s.at[then], d.at[then], p.at[then], e.at[then])

        def step(it, carry):
            for half in range(2):
                one(2 * it + half, half, (1, 2, 3))
            return carry

        one(0, 0, (1,))
        one(1, 1, (1, 2))
        lax.fori_loop(1, count // 2, step, 0)
        one(count, 0, (2, 3))
        one(count + 1, 1, (3,))

    def diag(q_ref, g_ref, x_ref, k_ref, v_ref, dq_ref, q, c, own):
        here = span(own)
        places = [pl.multiple_of(own * GROUP + b * BLK, BLK) for b in range(4)]
        query, grad = q_ref[span(q), :], g_ref[span(q), :]
        score = jnp.dot(k_ref[here, :], query.T, preferred_element_type=F32)
        dprob = jnp.dot(v_ref[here, :], grad.T, preferred_element_type=F32)
        norm, dot = lanes(x_ref, q, 0), lanes(x_ref, q, 1)
        probs, scores = [], []
        key_at = lax.broadcasted_iota(jnp.int32, (BLK, GROUP), 0)
        query_at = lax.broadcasted_iota(jnp.int32, (BLK, GROUP), 1)
        for i in range(4):
            bias = jnp.concatenate(
                [
                    jnp.full((1, BLK), jnp.where(table[4 * c + b, 32 + i] > 0, 0.0, FAR), F32)
                    for b in range(4)
                ],
                axis=1,
            )
            hide = (query_at >= i * BLK) & (query_at < key_at + i * BLK)
            cut = slice(i * BLK, (i + 1) * BLK)
            prob, score_e = soften(score[cut], dprob[cut], norm + bias, dot, hide)
            probs.append(prob)
            scores.append(score_e)
        prob = jnp.concatenate(probs, axis=0)
        score = jnp.concatenate(scores, axis=0)
        dk = jnp.dot(score, query, preferred_element_type=F32)
        dv = jnp.dot(prob, grad, preferred_element_type=F32)
        if isinstance(own, int):
            acc_k[own][...] += dk
            acc_v[own][...] += dv
        else:
            for i in range(4):
                @pl.when(own == i)
                def _(i=i):
                    acc_k[i][...] += dk
                    acc_v[i][...] += dv
        dq = jnp.dot(blocks(kt_ref, places, 1), score, preferred_element_type=F32)
        dq_ref[span(q), :] = (dq_ref[span(q), :].astype(F32) + (dq * SCALE).T).astype(BF)

    def clear(n):
        for ref in (*acc_k[:n], *acc_v[:n]):
            ref[...] = jnp.zeros((GROUP, BLK), F32)

    clear(8)

    def index_a(q):
        quad, xq = q // 4, q % 4
        zc = jnp.where(quad % 2 == 0, z, zq)
        kc = jnp.where(quad < 2, k, 1 - k)
        return xq * 8 + zc * 2 + kc

    loads[0].wait()
    turn(ka, 32)
    for load in loads[1:5]:
        load.wait()
    for load in loads[5:]:
        load.start()
    main(qa, ga, xa, ka, va, dqa, 16, index_a, [(0, lambda i: i * 8 + z * 2 + k), (4, lambda i: i * 8 + zk * 2 + k)])

    late = pl.ds(4 * GROUP, 12 * GROUP)
    store(dqa.at[late, :], dqa_out.at[late, :])

    for q in range(4):
        diag(qa, ga, xa, ka, va, dqa, q, index_a(q), q)
    early = pl.ds(0, 4 * GROUP)
    store(dqa.at[early, :], dqa_out.at[early, :])
    finish(dka, dva, 8)
    store(dka, dka_out)
    store(dva, dva_out)
    for load in loads[5:]:
        load.wait()

    clear(4)
    turn(kb, 16)
    main(qb, gb, xb, kb, vb, dqb, 8, lambda q: x * 8 + (q % 4) * 2 + q // 4, [(0, lambda i: i * 8 + z * 2 + k)])
    diag(qb, gb, xb, kb, vb, dqb, k * 4 + z, x * 8 + z * 2 + k, x)
    store(dqb, dqb_out)
    finish(dkb, dvb, 4)
    store(dkb, dkb_out)
    store(dvb, dvb_out)
    for copy in stores:
        copy.wait()


def compute_call(table, *gathered):
    wide = lambda n: jax.ShapeDtypeStruct((n * BLK, BLK), BF)
    any_ = pl.BlockSpec(memory_space=HBM)
    hold = lambda n: VMEM((n * BLK, BLK), BF)
    aux = lambda n: VMEM((n, 8, BLK), F32)
    return pl.pallas_call(
        compute_kernel,
        out_shape=(wide(64), wide(32), wide(32), wide(32), wide(16), wide(16)),
        in_specs=[pl.BlockSpec(memory_space=pltpu.SMEM)] + [any_] * 10,
        out_specs=(any_,) * 6,
        scratch_shapes=[
            hold(64), hold(64), aux(64), hold(32), hold(32), hold(32), hold(32), aux(32), hold(16), hold(16),
            hold(64), hold(32), hold(32), hold(32), hold(16), hold(16),
            pltpu.SemaphoreType.DMA((10,)), pltpu.SemaphoreType.DMA((7,)),
            [VMEM((GROUP, BLK), F32)] * 8, [VMEM((GROUP, BLK), F32)] * 8, hold(32),
            VMEM((2, 8 * BLK, GROUP), F32), VMEM((2, 8 * BLK, GROUP), F32),
            VMEM((2, 8 * BLK, GROUP), BF), VMEM((2, 8 * BLK, GROUP), BF),
        ],
        compiler_params=pltpu.CompilerParams(vmem_limit_bytes=VMEM_LIMIT),
        name="block_grads",
    )(table, *gathered)


def return_kernel(
    dqa, dka, dva, dqb, dkb, dvb,
    dq_out, dk_out, dv_out,
    own_q, own_k, own_v, own_bq, own_bk, own_bv, own_sem,
    got_zk, got_c, got_zq, put_zq, fin, bgot_c, bput_q, bgot_z, bgot_x, bfin,
    s_zk, r_zk, s_c, r_c, s_zq, r_zq, s_bc, r_bc, s_bz, r_bz, s_bx, r_bx, s_out, r_out,
):
    x, z, k, y = coords()
    outs = (dq_out, dk_out, dv_out)
    to_q = dev(x, q_pair(z), k, y)
    to_k = dev(x, k_pair(z), k, y)
    to_c = dev(x, z, 1 - k, y)
    half, quarter = pl.ds(0, 4 * GROUP), rows(x * GROUP, GROUP)
    loads = [
        pltpu.make_async_copy(src, dst, own_sem.at[i])
        for i, (src, dst) in enumerate([
            (dqa.at[pl.ds(0, 8 * GROUP), :], own_q),
            (dqb.at[rows(k * 4 * GROUP, 4 * GROUP), :], own_bq),
            (dka.at[half, :], own_k), (dva.at[half, :], own_v),
            (dkb.at[quarter, :], own_bk), (dvb.at[quarter, :], own_bv),
        ])
    ]
    for load in loads:
        load.start()
    greet()

    def chunk(ref, quad, dx):
        return ref.at[rows((quad * 4 + (x + dx) % 4) * GROUP, GROUP), :]

    def slab(ref, index):
        return ref.at[rows(index * GROUP, GROUP), :]

    def add(*refs):
        total = refs[0][...].astype(F32)
        for ref in refs[1:]:
            total = total + ref[...].astype(F32)
        return total.astype(BF)

    def give(n, src, base, tx, head_of, dx):
        for dy in range(4):
            ty = (y + dy) % 4
            block = src.at[rows(base + ty * BLK, BLK), :]
            dst = outs[n].at[:, cols(head_of)]
            if dx or dy:
                send(block, dst, s_out.at[n], r_out.at[n], dev(tx, z, k, ty))
            else:
                pltpu.make_async_copy(block, dst, r_out.at[n]).start()

    def keys_out(dx):
        for n, src in enumerate((dka, dva)):
            send(chunk(src, 1, dx), chunk(got_zk.at[n], 0, dx), s_zk, r_zk.at[n, dx], to_k)

    def far_keys_out(dx):
        for n, src in enumerate((dkb, dvb)):
            to = dev((x + dx) % 4, z, k, y)
            send(slab(src, (x + dx) % 4), slab(bgot_x.at[n], dx - 1), s_bx, r_bx.at[n, dx - 1], to)

    def queries_on(dx):
        wait(chunk(got_c, 1, dx), r_c.at[1, dx])
        part = chunk(put_zq, 0, dx)
        part[...] = add(chunk(own_q, 1, dx), chunk(got_c, 1, dx))
        send(part, chunk(got_zq, 0, dx), s_zq, r_zq.at[dx], to_q)

    def far_queries_on(dz):
        zt = (z + dz) % 4
        part = slab(bput_q, zt)
        part[...] = add(slab(own_bq, zt), slab(bgot_c, zt))
        send(part, slab(bgot_z, dz - 1), s_bz, r_bz.at[dz - 1], dev(x, zt, k, y))

    def keys_home(dx):
        tx = (x + dx) % 4
        for n, own in ((1, own_k), (2, own_v)):
            wait(chunk(got_zk.at[n - 1], 0, dx), r_zk.at[n - 1, dx])
            out = chunk(fin.at[n], 0, dx)
            out[...] = add(chunk(own, 0, dx), chunk(got_zk.at[n - 1], 0, dx))
            give(n, fin.at[n], tx * GROUP, tx, y * 4 + x, dx)

    def queries_home(dx):
        tx = (x + dx) % 4
        wait(chunk(got_c, 0, dx), r_c.at[0, dx])
        wait(chunk(got_zq, 0, dx), r_zq.at[dx])
        out = chunk(fin.at[0], 0, dx)
        out[...] = add(chunk(own_q, 0, dx), chunk(got_c, 0, dx), chunk(got_zq, 0, dx))
        give(0, fin.at[0], tx * GROUP, tx, y * 4 + x, dx)

    def far_keys_home():
        for n, own in ((1, own_bk), (2, own_bv)):
            for i in range(3):
                wait(slab(bgot_x.at[n - 1], i), r_bx.at[n - 1, i])
            bfin[n] = add(own, *[slab(bgot_x.at[n - 1], i) for i in range(3)])
            give(n, bfin.at[n], 0, x, 16 + y, 0)

    def far_queries_home():
        for i in range(3):
            wait(slab(bgot_z, i), r_bz.at[i])
        bfin[0] = add(slab(own_bq, z), slab(bgot_c, z), *[slab(bgot_z, i) for i in range(3)])
        give(0, bfin.at[0], 0, x, 16 + y, 0)

    first, second, third, last = ORDER
    for dx in ORDER:
        send(chunk(dqa, 3, dx), chunk(got_c, 1, dx), s_c, r_c.at[1, dx], to_c)
    send(dqb.at[rows((1 - k) * 4 * GROUP, 4 * GROUP), :], bgot_c, s_bc, r_bc, to_c)
    keys_out(first)
    far_keys_out(1)
    far_keys_out(3)
    for load in loads:
        load.wait()
    for dx in ORDER:
        send(chunk(dqa, 2, dx), chunk(got_c, 0, dx), s_c, r_c.at[0, dx], to_c)
    for dx in ORDER:
        queries_on(dx)
    far_keys_out(2)
    for dx in ORDER[1:]:
        keys_out(dx)
    wait(bgot_c, r_bc)
    for dz in (1, 3, 2):
        far_queries_on(dz)
    for dx in ORDER:
        queries_home(dx)
        keys_home(dx)
        if dx == 1:
            far_keys_home()
    far_queries_home()

    for n in range(3):
        wait(outs[n], r_out.at[n])
        wait(dqa.at[pl.ds(0, 18 * BLK), :], s_out.at[n])
    wait(dqa.at[pl.ds(0, 8 * GROUP), :], s_c)
    wait(dqa.at[pl.ds(0, 8 * GROUP), :], s_zk)
    wait(put_zq, s_zq)
    wait(bgot_c, s_bc)
    wait(bgot_z, s_bz)
    wait(dqa.at[pl.ds(0, 6 * GROUP), :], s_bx)


def hand_out_kernel(dq, dk, dv, dq_out, dk_out, dv_out, held, sems):
    part = dq.shape[0] // SPLIT
    pieces = [(n, i) for i in range(SPLIT) for n in range(3)]
    src, dst = (dq, dk, dv), (dq_out, dk_out, dv_out)

    def cut(ref, i):
        return ref.at[pl.ds(i * part, part), :]

    loads = [pltpu.make_async_copy(cut(src[n], i), cut(held.at[n], i), sems.at[0, n, i]) for n, i in pieces]
    stores = [pltpu.make_async_copy(cut(held.at[n], i), cut(dst[n], i), sems.at[1, n, i]) for n, i in pieces]
    for load in loads:
        load.start()
    for load, store in zip(loads, stores):
        load.wait()
        store.start()
    for store in stores:
        store.wait()


def body(queries, key_rows, value_rows, forward_out, out_grad, log_norm, block_order, pattern):
    wide = lambda n: jax.ShapeDtypeStruct((n * BLK, BLK), BF)
    aux = lambda n: jax.ShapeDtypeStruct((n, 8, BLK), F32)
    any_ = pl.BlockSpec(memory_space=HBM)
    vmem = pl.BlockSpec(memory_space=VMEM)
    sem = lambda *shape: pltpu.SemaphoreType.DMA(shape)
    one = pltpu.SemaphoreType.DMA
    hold = lambda n: VMEM((n * BLK, BLK), BF)
    tokens, width = queries.shape

    gathered = pl.pallas_call(
        gather_kernel,
        out_shape=(
            wide(64), wide(64), aux(64), wide(32), wide(32),
            wide(32), wide(32), aux(32), wide(16), wide(16),
            jax.ShapeDtypeStruct((BLK, BLK), jnp.int32),
        ),
        in_specs=[any_] * 5 + [vmem] * 3,
        out_specs=(any_,) * 10 + (vmem,),
        scratch_shapes=[
            VMEM((tokens, width), BF), VMEM((tokens, width), BF), VMEM((HEADS, 8, BLK), F32),
            VMEM((BLK, BLK), F32), VMEM((8, BLK, BLK), BF), sem(8),
            sem(2), sem(5), sem(5, 4), sem(5), sem(5), sem(5), sem(5, 4), sem(5), sem(5), sem(5), sem(5), sem(2), sem(2),
            sem(5), sem(5, 4), sem(5), sem(5), sem(2), sem(2, 4),
        ],
        compiler_params=pltpu.CompilerParams(
            collective_id=0, has_side_effects=True, vmem_limit_bytes=VMEM_LIMIT
        ),
        name="gather_blocks",
    )(
        queries, key_rows, value_rows, out_grad, forward_out, log_norm.T, pattern.T,
        block_order.reshape(1, BLK),
    )
    table = gathered[-1]

    grads = compute_call(table, *gathered[:10])
    flat = jax.ShapeDtypeStruct((tokens, width), BF)
    landed = pl.pallas_call(
        return_kernel,
        out_shape=(flat, flat, flat),
        in_specs=[any_] * 6,
        out_specs=(any_,) * 3,
        scratch_shapes=[
            hold(32), hold(16), hold(16), hold(16), hold(4), hold(4), sem(6),
            VMEM((2, 16 * BLK, BLK), BF), VMEM((32 * BLK, BLK), BF), VMEM((16 * BLK, BLK), BF),
            VMEM((16 * BLK, BLK), BF), VMEM((3, 16 * BLK, BLK), BF),
            VMEM((16 * BLK, BLK), BF), VMEM((16 * BLK, BLK), BF), VMEM((12 * BLK, BLK), BF),
            VMEM((2, 12 * BLK, BLK), BF), VMEM((3, GROUP, BLK), BF),
            one, sem(2, 4), one, sem(2, 4), one, sem(4), one, one, one, sem(3), one, sem(2, 3), sem(3), sem(3),
        ],
        compiler_params=pltpu.CompilerParams(
            collective_id=1, has_side_effects=True, vmem_limit_bytes=VMEM_LIMIT
        ),
        name="return_grads",
    )(*grads)
    return pl.pallas_call(
        hand_out_kernel,
        out_shape=(flat, flat, flat),
        in_specs=[any_] * 3,
        out_specs=(any_,) * 3,
        scratch_shapes=[VMEM((3, tokens, width), BF), sem(2, 3, SPLIT)],
        compiler_params=pltpu.CompilerParams(vmem_limit_bytes=VMEM_LIMIT),
        name="hand_out",
    )(*landed)


def solution(mesh):
    tokens = P(("ctx", "head"), None)
    return jax.shard_map(
        body,
        mesh=mesh,
        in_specs=(tokens,) * 6 + (P(), P()),
        out_specs=(tokens,) * 3,
        check_vma=False,
    )
```
